512 devices in a mesh: gx: 8 (over x, core), gy: 8 (over z), vert: 8 (over y).
Axes of the slice: x: 4, y: 8, z: 8, core: 2. Of those that a mesh axis runs over, the one named last changes fastest.
Arguments:
- distribution: bfloat16 [64, 16, 24, 4608], P('gx', 'gy', 'vert'), may hold values from 0.049804688 to 2
- wall_mask: int32 [64, 16], replicated, may hold values from 0 to 2
- pair_table: int32 [8, 8], replicated, may hold values from 0 to 7
- trans_weight: float32 [8], replicated, may hold values from 0.02 to 0.25
- kernels: float32 [5, 13824], replicated, as said below
Outputs:
- new_distribution: bfloat16 [64, 16, 24, 4608], P('gx', 'gy', 'vert')
The draws below stay inside these ranges and needn't reach their ends.
Inputs may be any that keep to these rules, and one draw needn't show every extreme that they name: `wall_mask`: 0 marks a fluid cell, 1 a solid cell, 2 a cut cell at the wall. `pair_table`: indexes trans_weight. `kernels`: every entry is positive, and each row is even in each mode index separately: unchanged when the x mode a becomes (24 - a) mod 24, and likewise for the y and z modes.
All inputs are finite; a program needn't handle non-finite values.
Results may differ from the reference program's by a relative error of at most 0.001.
The reference program's roundings to bfloat16 on the way (of `transported`) count: a program that leaves them out, or rounds other values in their place, can miss the bound.
Values may be sent and summed in bfloat16 or wider, within the bound.
No kernel may reach another device: no remote copies, remote signals or barrier semaphores. Data moves between devices by JAX's collectives and lax.ppermute only.
A program may use at most 64 MiB of HBM per device.

```python
import math
import jax
import jax.numpy as jnp
from jax import lax

VX = 24
VY = 24
VZ = 24
LEVELS = 8
DIRS = 2
NTAB = 8
KERNELS = 5
NX = 64
NY = 16


def draw_kernels(key, part):
    fold_x = jnp.minimum(jnp.arange(VX, dtype=jnp.int32), VX - jnp.arange(VX, dtype=jnp.int32))
    fold_y = jnp.minimum(jnp.arange(VY, dtype=jnp.int32), VY - jnp.arange(VY, dtype=jnp.int32))
    fold_z = jnp.minimum(jnp.arange(VZ, dtype=jnp.int32), VZ - jnp.arange(VZ, dtype=jnp.int32))
    layout = (KERNELS, VX // 2 + 1, VY // 2 + 1, VZ // 2 + 1)
    base_values = jax.random.uniform(key, layout, jnp.float32, 0.5, 1.5)
    rough = base_values[:, fold_x][:, :, fold_y][:, :, :, fold_z]
    radius = (fold_x[:, None, None] ** 2 + fold_y[None, :, None] ** 2 + fold_z[None, None, :] ** 2).astype(jnp.float32)
    envelope = 1.0 / (1.0 + radius / (VX * VX / 16.0))
    return (rough * envelope[None]).reshape(KERNELS, VX * VY * VZ)


def with_ends(drawn, rng, smallest, largest):
    dims = drawn.shape
    index_at = [jax.random.randint(jax.random.fold_in(rng, axis), (), 0, dims[axis]) for axis in range(len(dims))]
    drawn = drawn.at[tuple(index_at)].set(smallest)
    longest = dims.index(max(dims))
    index_at[longest] = (index_at[longest] + 1) % dims[longest]
    return drawn.at[tuple(index_at)].set(largest)


def block_levels(key, dims, pieces, smallest, largest):
    gain = 1.0
    for axis_at, shards_of in pieces:
        steps = jax.random.uniform(jax.random.fold_in(jax.random.fold_in(key, 6), axis_at), (shards_of,), jnp.float32, smallest / len(pieces), largest / len(pieces))
        gain = gain * jnp.repeat(jnp.exp(steps), dims[axis_at] // shards_of).reshape((-1,) + (1,) * (len(dims) - 1 - axis_at))
    return gain


def setup_inputs(seed: int = 0) -> dict:
    seeds = jax.random.split(jax.random.key(seed), 6)
    distribution = jnp.clip(jnp.exp(math.log(2.0) - 3.6927934 * jax.random.uniform(seeds[0], (NX, NY, VX, LEVELS * VY * VZ), jnp.float32) ** block_levels(seeds[0], (NX, NY, VX, LEVELS * VY * VZ), ((0, 8), (1, 8), (2, 8)), -0.2, 0.2)), 0.049804688, 2.0).astype(jnp.bfloat16)
    wall_mask = with_ends(jax.random.randint(seeds[1], (NX, NY), 0, 3), jax.random.fold_in(seeds[1], 1), 0, 2).astype(jnp.int32)
    pair_table = with_ends(jax.random.randint(seeds[2], (LEVELS, LEVELS), 0, NTAB), jax.random.fold_in(seeds[2], 1), 0, NTAB - 1).astype(jnp.int32)
    trans_weight = jnp.clip(jnp.exp(jax.random.uniform(seeds[3], (NTAB,), jnp.float32, math.log(0.02), math.log(0.25))), 0.02, 0.25)
    kernels = draw_kernels(jax.random.fold_in(seeds[5], 71), 0)
    return {"distribution": distribution, "wall_mask": wall_mask, "pair_table": pair_table, "trans_weight": trans_weight, "kernels": kernels}


courant = 0.45
collide_step = 0.4
highest = lax.Precision.HIGHEST


def slab_cut(values, start, stop, axis):
    return lax.slice_in_dim(values, start, stop, axis=axis)


def flux_update(padded, face_weight, speeds, axis):
    extent = padded.shape[axis] - 4
    lower_diff = slab_cut(padded, 1, extent + 3, axis) - slab_cut(padded, 0, extent + 2, axis)
    upper_diff = slab_cut(padded, 2, extent + 4, axis) - slab_cut(padded, 1, extent + 3, axis)
    slopes = 0.5 * (jnp.sign(lower_diff) + jnp.sign(upper_diff)) * jnp.minimum(jnp.abs(lower_diff), jnp.abs(upper_diff))
    from_left = slab_cut(padded, 1, extent + 2, axis) + 0.5 * (1.0 - speeds) * slab_cut(slopes, 0, extent + 1, axis)
    from_right = slab_cut(padded, 2, extent + 3, axis) - 0.5 * (1.0 + speeds) * slab_cut(slopes, 1, extent + 2, axis)
    fluxes = face_weight * (jnp.maximum(speeds, 0.0) * from_left + jnp.minimum(speeds, 0.0) * from_right)
    return slab_cut(fluxes, 0, extent, axis) - slab_cut(fluxes, 1, extent + 1, axis)


def open_share(wall_mask):
    return jnp.where(wall_mask == 1, 0.0, jnp.where(wall_mask == 2, 0.5, 1.0)).astype(jnp.float32)


def velocity_speeds(row_width):
    index_y = (jnp.arange(row_width, dtype=jnp.int32) // VZ) % VY
    return courant * (2.0 * index_y.astype(jnp.float32) - (VY - 1)) / (VY - 1)


def wrap_pad(values, axis):
    extent = values.shape[axis]
    return jnp.concatenate([slab_cut(values, extent - 2, extent, axis), values, slab_cut(values, 0, 2, axis)], axis=axis)


def reference(distribution, wall_mask, pair_table, trans_weight, kernels):
    openness = open_share(wall_mask)
    cycle_x = jnp.concatenate([openness[-1:], openness, openness[:1]], axis=0)
    face_x = jnp.minimum(cycle_x[:-1], cycle_x[1:])[:, :, None]
    cycle_y = jnp.concatenate([openness[:, -1:], openness, openness[:, :1]], axis=1)
    face_y = jnp.minimum(cycle_y[:, :-1], cycle_y[:, 1:])[:, :, None]
    row_width = distribution.shape[3]
    speeds_y = velocity_speeds(row_width).reshape(1, 1, row_width)
    index_x = jnp.arange(VX, dtype=jnp.int32).astype(jnp.float32)
    speeds_x = courant * (2.0 * index_x - (VX - 1)) / (VX - 1)
    planes = jnp.moveaxis(distribution, 2, 0)

    def transport(inputs):
        plane_data, speed_x = inputs
        values = plane_data.astype(jnp.float32)
        change_x = flux_update(wrap_pad(values, 0), face_x, speed_x, 0)
        change_y = flux_update(wrap_pad(values, 1), face_y, speeds_y, 1)
        return (values + change_x + change_y).astype(jnp.bfloat16)

    transported = lax.map(transport, (planes, speeds_x))
    cell_rows = jnp.transpose(transported.reshape(VX, NX * NY, row_width), (1, 0, 2))
    entries = jnp.arange(trans_weight.shape[0], dtype=jnp.int32)
    mixing = jnp.sum(jnp.where(pair_table[:, :, None] == entries[None, None, :], trans_weight[None, None, :], 0.0), axis=-1)
    kernel_cube = kernels.reshape(KERNELS, VX, VY, VZ)
    cube_axes = (1, 2, 3)

    def collide(inputs):
        cell_data, cell_open = inputs
        fields = jnp.transpose(cell_data.astype(jnp.float32).reshape(VX, LEVELS, VY, VZ), (1, 0, 2, 3))
        mixed_levels = jnp.einsum("lm,mxyz->lxyz", mixing, fields, precision=highest)
        spectrum = jnp.fft.fftn(fields, axes=cube_axes)
        mixed_spectrum = jnp.fft.fftn(mixed_levels, axes=cube_axes)
        gain_term = jnp.zeros_like(fields)
        for direction in range(DIRS):
            gain_left = jnp.real(jnp.fft.ifftn(kernel_cube[direction] * spectrum, axes=cube_axes))
            gain_right = jnp.real(jnp.fft.ifftn(kernel_cube[DIRS + direction] * mixed_spectrum, axes=cube_axes))
            gain_term = gain_term + gain_left * gain_right
        loss_term = jnp.real(jnp.fft.ifftn(kernel_cube[2 * DIRS] * mixed_spectrum, axes=cube_axes))
        collision = gain_term - fields * loss_term
        updated = fields + collide_step * cell_open * collision
        return jnp.transpose(updated, (1, 0, 2, 3)).reshape(VX, row_width).astype(jnp.bfloat16)

    result = lax.map(collide, (cell_rows, openness.reshape(NX * NY)))
    return result.reshape(NX, NY, VX, row_width)
```

```python
import math

import numpy as np
import jax
import jax.numpy as jnp
from jax import lax
from jax.experimental import pallas as pl
from jax.experimental.pallas import tpu as pltpu
from jax.sharding import PartitionSpec as P

VX = 24
VY = 24
VZ = 24
LEVELS = 8
PLANE = VY * VZ
HALF = PLANE // 2
SUB = 3
LANES = SUB * HALF
WIDE = 896

courant = 0.45
collide_step = 0.4
high = lax.Precision.HIGH


def open_share(wall_mask):
    return jnp.where(wall_mask == 1, 0.0, jnp.where(wall_mask == 2, 0.5, 1.0)).astype(jnp.float32)


def cas_matrix(extent):
    counter = np.arange(extent)
    angles = (np.outer(counter, counter) % extent) * (2.0 * np.pi / extent)
    return np.cos(angles) + np.sin(angles)


def speed(index):
    return courant * (2.0 * index - (VX - 1)) / (VX - 1)


def lane_speeds():
    rows = []
    for half in range(2):
        j = np.arange(HALF) // VZ + half * (VY // 2)
        row = np.zeros((WIDE,), np.float32)
        row[:LANES] = np.tile(np.abs(speed(j)), SUB)
        rows.append(np.broadcast_to(row, (LEVELS, WIDE)))
    return np.stack(rows).astype(np.float32)


def minmod(a, b):
    return jnp.maximum(jnp.minimum(a, b), jnp.minimum(jnp.maximum(a, b), 0.0))


def transport_kernel(flags, face_x, face_y, own, xup, xdn, low, high_, speeds_x, speeds_y, out):
    rows_x = own.shape[1]
    forward = flags[0] > 0

    def pick(step):
        return jnp.where(forward, step, rows_x - 1 - step)

    def tile(t, carry):
        lanes = pl.ds(pl.multiple_of(t * 128, 128), 128)
        nu_x = speeds_x[:, lanes]
        half_x = 0.5 * (1.0 - nu_x)
        for half in range(2):
            nu_y = speeds_y[half, :, lanes]
            half_y = 0.5 * (1.0 - nu_y)
            first, second = (0, 1) if half == 1 else (1, 0)

            def f32(ref, *at):
                return ref[at[0], at[1], :, lanes].astype(jnp.float32)

            prev = []
            for y in range(2):
                q = 2 * y + half
                far = f32(xup, q, 0)
                near = f32(xup, q, 1)
                now = f32(own, q, pick(0))
                slope = minmod(near - far, now - near)
                flux = face_x[0, y] * (nu_x * (near + half_x * slope))
                prev.append((now, now - near, flux))
            for step in range(rows_x):
                row = pick(step)
                changed = []
                values = []
                for y in range(2):
                    q = 2 * y + half
                    now, diff, flux = prev[y]
                    if step + 1 < rows_x:
                        nxt = f32(own, q, pick(step + 1))
                    else:
                        nxt = f32(xdn, q, 0)
                    later = nxt - now
                    flux_out = face_x[step + 1, y] * (
                        nu_x * (now + half_x * minmod(diff, later))
                    )
                    changed.append(now + (flux - flux_out))
                    values.append(now)
                    prev[y] = (nxt, later, flux_out)
                if half == 1:
                    up2, up1, down = f32(low, 0, row), f32(low, 1, row), f32(high_, 2, row)
                else:
                    up2, up1, down = f32(high_, 1, row), f32(high_, 0, row), f32(low, 2, row)
                a, b = values[first], values[second]
                d0, d1, d2, d3 = up1 - up2, a - up1, b - a, down - b
                w0, w1, w2 = (0, 1, 2) if half == 1 else (2, 1, 0)
                g0 = face_y[row, w0] * (nu_y * (up1 + half_y * minmod(d0, d1)))
                g1 = face_y[row, w1] * (nu_y * (a + half_y * minmod(d1, d2)))
                g2 = face_y[row, w2] * (nu_y * (b + half_y * minmod(d2, d3)))
                out[row, 2 * first + half, :, lanes] = (changed[first] + (g0 - g1)).astype(
                    jnp.bfloat16
                )
                out[row, 2 * second + half, :, lanes] = (changed[second] + (g1 - g2)).astype(
                    jnp.bfloat16
                )
        return carry

    lax.fori_loop(0, WIDE // 128, tile, 0)


def transport(flag, face_x, face_y, own, xup, xdn, low, high_, speeds_x, speeds_y):
    rows_x = own.shape[1]
    smem = pl.BlockSpec(memory_space=pltpu.SMEM)
    vmem = pl.BlockSpec(memory_space=pltpu.VMEM)
    return pl.pallas_call(
        transport_kernel,
        out_shape=jax.ShapeDtypeStruct((rows_x, 4, LEVELS, WIDE), jnp.bfloat16),
        in_specs=[smem] * 3 + [vmem] * 7,
        out_specs=vmem,
        compiler_params=pltpu.CompilerParams(vmem_limit_bytes=32 * 1024 * 1024),
        cost_estimate=pl.CostEstimate(flops=10_000_000, bytes_accessed=2_000_000, transcendentals=0),
    )(flag, face_x, face_y, own, xup, xdn, low, high_, speeds_x, speeds_y)


def transform(fields, table_x, table_yz):
    partial_x = jnp.einsum("ab,nblc->nalc", table_x, fields, precision=high)
    return jnp.einsum("nalc,cd->nald", partial_x, table_yz, precision=high)


def ring(count, step):
    return [(i, (i + step) % count) for i in range(count)]


def body(distribution, wall_mask, pair_table, trans_weight, kernels):
    rows_x, rows_y, local_vx, row_width = distribution.shape
    count_x = lax.axis_size("gx")
    count_y = lax.axis_size("gy")
    count_v = lax.axis_size("vert")
    at_v = lax.axis_index("vert")
    forward = at_v >= count_v // 2

    own = distribution.reshape(rows_x, 2, SUB, LEVELS, 2, HALF)
    own = own.transpose(1, 4, 0, 3, 2, 5).reshape(4, rows_x, LEVELS, LANES)
    own = jnp.pad(own, ((0, 0), (0, 0), (0, 0), (0, WIDE - LANES)))

    low = lax.ppermute(jnp.stack([own[1], own[3], own[2]]), "gy", ring(count_y, 1))
    high_ = lax.ppermute(jnp.stack([own[0], own[2], own[1]]), "gy", ring(count_y, -1))
    upstream = jnp.where(forward, own[:, rows_x - 2 :], own[:, 1::-1])
    downstream = jnp.where(forward, own[:, :1], own[:, rows_x - 1 :])
    send_up, send_down = [], []
    for i in range(count_x):
        for v in range(count_v):
            step = 1 if v >= count_v // 2 else -1
            send_up.append((i * count_v + v, (i + step) % count_x * count_v + v))
            send_down.append((i * count_v + v, (i - step) % count_x * count_v + v))
    xup = lax.ppermute(upstream, ("gx", "vert"), send_up)
    xdn = lax.ppermute(downstream, ("gx", "vert"), send_down)

    openness = open_share(wall_mask)
    wrapped = jnp.pad(openness, 1, mode="wrap")
    anchor_x = lax.axis_index("gx") * rows_x
    anchor_y = lax.axis_index("gy") * rows_y
    window = lax.dynamic_slice(wrapped, (anchor_x, anchor_y), (rows_x + 2, rows_y + 2))
    open_x = window[:, 1 : rows_y + 1]
    face_x = jnp.minimum(open_x[:-1], open_x[1:])
    face_x = jnp.where(forward, face_x, face_x[::-1])
    open_y = window[1 : rows_x + 1]
    face_y = jnp.minimum(open_y[:, :-1], open_y[:, 1:])
    own_open = lax.dynamic_slice(openness, (anchor_x + at_v, anchor_y), (1, rows_y))[0]

    index_x = at_v * local_vx + jnp.arange(WIDE, dtype=jnp.int32) // HALF
    speeds_x = jnp.abs(speed(index_x.astype(jnp.float32)))
    speeds_x = jnp.broadcast_to(speeds_x[None], (LEVELS, WIDE))
    speeds_y = jnp.asarray(lane_speeds())
    flag = forward.astype(jnp.int32).reshape(1)
    transported = transport(flag, face_x, face_y, own, xup, xdn, low, high_, speeds_x, speeds_y)

    block = lax.all_to_all(transported, "vert", split_axis=0, concat_axis=0, tiled=True)
    fields = block[..., :LANES].reshape(count_v, 2, 2, LEVELS, SUB, HALF)
    fields = fields.transpose(1, 0, 4, 3, 2, 5).reshape(2, VX, LEVELS, PLANE).astype(jnp.float32)

    entries = jnp.arange(trans_weight.shape[0], dtype=jnp.int32)
    mixing = jnp.sum(
        jnp.where(
            pair_table[:, :, None] == entries[None, None, :], trans_weight[None, None, :], 0.0
        ),
        axis=-1,
    )
    table_x = jnp.asarray(cas_matrix(VX).astype(np.float32))
    table_yz = jnp.asarray(np.kron(cas_matrix(VY), cas_matrix(VZ)).astype(np.float32))
    bank = kernels.reshape(kernels.shape[0], VX, 1, PLANE) / float(VX * PLANE)
    spectrum = transform(fields, table_x, table_yz)
    mixed_spectrum = jnp.einsum("lm,namc->nalc", mixing, spectrum, precision=high)
    gain_term = jnp.zeros_like(fields)
    for direction in range(2):
        gain_left = transform(bank[direction] * spectrum, table_x, table_yz)
        gain_right = transform(bank[2 + direction] * mixed_spectrum, table_x, table_yz)
        gain_term = gain_term + gain_left * gain_right
    loss_term = transform(bank[4] * mixed_spectrum, table_x, table_yz)
    collision = gain_term - fields * loss_term
    weights = own_open.reshape(2, 1, 1, 1)
    updated = (fields + collide_step * weights * collision).astype(jnp.bfloat16)
    updated = updated.reshape(1, 2, VX, row_width)
    return lax.all_to_all(updated, "vert", split_axis=2, concat_axis=0, tiled=True)


def solution(mesh):
    in_specs = (P("gx", "gy", "vert", None), P(), P(), P(), P())
    out_specs = P("gx", "gy", "vert", None)
    return jax.shard_map(body, mesh=mesh, in_specs=in_specs, out_specs=out_specs, check_vma=False)
```

```python
import math

import ml_dtypes
import numpy as np
import jax
import jax.numpy as jnp
from jax import lax
from jax.experimental import pallas as pl
from jax.experimental.pallas import tpu as pltpu
from jax.sharding import PartitionSpec as P

VX = 24
VY = 24
VZ = 24
LEVELS = 8
PLANE = VY * VZ
HALF = PLANE // 2
SUB = 3
LANES = SUB * HALF
WIDE = 896
YZ = 640
MAIN = 512
DEPTH = 3 * MAIN + 256

courant = 0.45
collide_step = 0.4


def open_share(wall_mask):
    return jnp.where(wall_mask == 1, 0.0, jnp.where(wall_mask == 2, 0.5, 1.0)).astype(jnp.float32)


def cas_matrix(extent):
    counter = np.arange(extent)
    angles = (np.outer(counter, counter) % extent) * (2.0 * np.pi / extent)
    return np.cos(angles) + np.sin(angles)


def speed(index):
    return courant * (2.0 * index - (VX - 1)) / (VX - 1)


def lane_speeds():
    rows = []
    for half in range(2):
        j = np.arange(HALF) // VZ + half * (VY // 2)
        row = np.zeros((WIDE,), np.float32)
        row[:LANES] = np.tile(np.abs(speed(j)), SUB)
        rows.append(np.broadcast_to(row, (LEVELS, WIDE)))
    return np.stack(rows).astype(np.float32)


def minmod(a, b):
    return jnp.maximum(jnp.minimum(a, b), jnp.minimum(jnp.maximum(a, b), 0.0))


def transport_kernel(flags, face_x, face_y, own, xup, xdn, low, high_, speeds_x, speeds_y, out):
    rows_x = own.shape[1]
    forward = flags[0] > 0

    def pick(step):
        return jnp.where(forward, step, rows_x - 1 - step)

    def tile(t, carry):
        lanes = pl.ds(pl.multiple_of(t * 128, 128), 128)
        nu_x = speeds_x[:, lanes]
        half_x = 0.5 * (1.0 - nu_x)
        for half in range(2):
            nu_y = speeds_y[half, :, lanes]
            half_y = 0.5 * (1.0 - nu_y)
            first, second = (0, 1) if half == 1 else (1, 0)

            def f32(ref, *at):
                return ref[at[0], at[1], :, lanes].astype(jnp.float32)

            prev = []
            for y in range(2):
                q = 2 * y + half
                far = f32(xup, q, 0)
                near = f32(xup, q, 1)
                now = f32(own, q, pick(0))
                slope = minmod(near - far, now - near)
                flux = face_x[0, y] * (nu_x * (near + half_x * slope))
                prev.append((now, now - near, flux))
            for step in range(rows_x):
                row = pick(step)
                changed = []
                values = []
                for y in range(2):
                    q = 2 * y + half
                    now, diff, flux = prev[y]
                    if step + 1 < rows_x:
                        nxt = f32(own, q, pick(step + 1))
                    else:
                        nxt = f32(xdn, q, 0)
                    later = nxt - now
                    flux_out = face_x[step + 1, y] * (
                        nu_x * (now + half_x * minmod(diff, later))
                    )
                    changed.append(now + (flux - flux_out))
                    values.append(now)
                    prev[y] = (nxt, later, flux_out)
                if half == 1:
                    up2, up1, down = f32(low, 0, row), f32(low, 1, row), f32(high_, 2, row)
                else:
                    up2, up1, down = f32(high_, 1, row), f32(high_, 0, row), f32(low, 2, row)
                a, b = values[first], values[second]
                d0, d1, d2, d3 = up1 - up2, a - up1, b - a, down - b
                w0, w1, w2 = (0, 1, 2) if half == 1 else (2, 1, 0)
                g0 = face_y[row, w0] * (nu_y * (up1 + half_y * minmod(d0, d1)))
                g1 = face_y[row, w1] * (nu_y * (a + half_y * minmod(d1, d2)))
                g2 = face_y[row, w2] * (nu_y * (b + half_y * minmod(d2, d3)))
                out[row, 2 * first + half, :, lanes] = (changed[first] + (g0 - g1)).astype(
                    jnp.bfloat16
                )
                out[row, 2 * second + half, :, lanes] = (changed[second] + (g1 - g2)).astype(
                    jnp.bfloat16
                )
        return carry

    lax.fori_loop(0, WIDE // 128, tile, 0)


def transport(flag, face_x, face_y, own, xup, xdn, low, high_, speeds_x, speeds_y):
    rows_x = own.shape[1]
    smem = pl.BlockSpec(memory_space=pltpu.SMEM)
    vmem = pl.BlockSpec(memory_space=pltpu.VMEM)
    return pl.pallas_call(
        transport_kernel,
        out_shape=jax.ShapeDtypeStruct((rows_x, 4, LEVELS, WIDE), jnp.bfloat16),
        in_specs=[smem] * 3 + [vmem] * 7,
        out_specs=vmem,
        compiler_params=pltpu.CompilerParams(vmem_limit_bytes=16 * 1024 * 1024),
        cost_estimate=pl.CostEstimate(flops=10_000_000, bytes_accessed=2_000_000, transcendentals=0),
    )(flag, face_x, face_y, own, xup, xdn, low, high_, speeds_x, speeds_y)


def small(matrix, inputs):
    products = {}

    def product(scale, n):
        if scale == 1.0:
            return inputs[n]
        if (scale, n) not in products:
            products[scale, n] = inputs[n] * scale
        return products[scale, n]

    results = []
    for row in matrix:
        total = None
        for n, value in enumerate(row):
            value = round(float(value), 12)
            if value == 0.0:
                continue
            term = product(abs(value), n)
            if total is None:
                total = term if value > 0 else -term
            else:
                total = total + term if value > 0 else total - term
        results.append(total)
    return results


def trig(function, outs, ins, over):
    return [[function(math.pi * k * n / over) for n in ins] for k in outs]


def cosines(v):
    e = [v[n] + v[12 - n] for n in range(6)] + [v[6]]
    o = [v[n] - v[12 - n] for n in range(6)]
    ee = [e[n] + e[6 - n] for n in range(3)] + [e[3]]
    eo = [e[n] - e[6 - n] for n in range(3)]
    out = [None] * 13
    out[0::4] = small(trig(math.cos, range(4), range(4), 3), ee)
    out[2::4] = small(trig(math.cos, (1, 3, 5), range(3), 6), eo)
    out[1::2] = small(trig(math.cos, (1, 3, 5, 7, 9, 11), range(6), 12), o)
    return out


def sines(v):
    v = [None] + v
    f = [v[n] + v[12 - n] for n in range(1, 6)] + [v[6]]
    g = [None] + [v[n] - v[12 - n] for n in range(1, 6)]
    gp = [g[1] + g[5], g[2] + g[4], g[3]]
    gm = [g[1] - g[5], g[2] - g[4]]
    out = [None] * 11
    out[0::2] = small(trig(math.sin, (1, 3, 5, 7, 9, 11), range(1, 7), 12), f)
    out[1::4] = small(trig(math.sin, (1, 3, 5), (1, 2, 3), 6), gp)
    out[3::4] = small(trig(math.sin, (2, 4), (1, 2), 6), gm)
    return out


def modes_of(x):
    even = [x[0]] + [x[n] + x[VX - n] for n in range(1, 12)] + [x[12]]
    odd = [x[n] - x[VX - n] for n in range(1, 12)]
    return cosines(even) + sines(odd)


def points_of(modes):
    p = cosines(modes[:13])
    q = sines(modes[13:])
    out = [None] * VX
    out[0], out[12] = p[0], p[12]
    for n in range(1, 12):
        out[n] = p[n] + q[n - 1]
        out[VX - n] = p[n] - q[n - 1]
    return out


def split_table():
    table = np.kron(cas_matrix(VY), cas_matrix(VZ)).astype(np.float32)
    table = np.pad(table, ((0, 0), (0, YZ - PLANE)))
    top = table.astype(ml_dtypes.bfloat16)
    low = (table - top.astype(np.float32)).astype(ml_dtypes.bfloat16)
    rest = PLANE - MAIN
    back = np.zeros((DEPTH, YZ), ml_dtypes.bfloat16)
    back[0:MAIN] = top[:MAIN]
    back[MAIN : 2 * MAIN] = top[:MAIN]
    back[2 * MAIN : 3 * MAIN] = low[:MAIN]
    back[3 * MAIN : 3 * MAIN + rest] = top[MAIN:PLANE]
    back[3 * MAIN + rest : 3 * MAIN + 2 * rest] = top[MAIN:PLANE]
    back[3 * MAIN + 128 : 3 * MAIN + 128 + rest] = low[MAIN:PLANE]
    return back


def collide_kernel(
    weights, block, bank, coefs, back, out, g, spec, mixed, lhs, left, gain
):
    cells = block.shape[1] // 2
    per_cell = VX * LEVELS
    blank = jnp.zeros((LEVELS, YZ - PLANE), jnp.float32)

    def plane(cell, a):
        source, i = a // SUB, a % SUB
        wide = [block[source, 2 * cell + half].astype(jnp.float32) for half in range(2)]
        cut = [part[:, i * HALF : (i + 1) * HALF] for part in wide]
        return jnp.concatenate(cut + [blank], axis=1)

    for cell in range(cells):
        for m in range(VX // 2):
            pair = jnp.concatenate([plane(cell, 2 * m), plane(cell, 2 * m + 1)], axis=0)
            at_rows = pl.ds(cell * per_cell + 2 * m * LEVELS, 2 * LEVELS)
            g[at_rows, :] = pair.astype(jnp.bfloat16)

    tiles = YZ // 128
    chunks = ((0, 256), (256, 256), (512, 128))

    edge = jnp.concatenate([g[:, MAIN:], g[:, MAIN:]], axis=1)
    for start, width in chunks:
        cols = pl.ds(start, width)
        total = jnp.dot(edge, back[3 * MAIN :, cols], preferred_element_type=jnp.float32)
        for first in (0, 2 * MAIN):
            total = total + jnp.dot(
                g[:, :MAIN], back[pl.ds(first, MAIN), cols], preferred_element_type=jnp.float32
            )
        spec[:, cols] = total

    def rows(base, a, count=LEVELS):
        return pl.ds(base + a * LEVELS, count)

    def ahead(index):
        base, lanes = index // tiles * per_cell, pl.ds(index % tiles * 128, 128)
        modes = modes_of([spec[rows(base, a), lanes] for a in range(VX)])
        for a in range(VX):
            total = coefs[0] * modes[a]
            for shift in range(1, LEVELS):
                total = total + coefs[shift] * pltpu.roll(modes[a], shift, 0)
            spec[rows(base, a), lanes] = modes[a]
            mixed[rows(base, a), lanes] = total

    for index in range(cells * tiles):
        ahead(index)

    lane = lax.broadcasted_iota(jnp.int32, (2 * LEVELS, 128), 1)

    def prepare(slot, which, source, base, lanes, t, last):
        factors = [bank[which, pl.ds(k, 1), lanes] for k in range(13)]
        points = points_of(
            [source[rows(base, a), lanes] * factors[a if a < 13 else a - 12] for a in range(VX)]
        )
        for m in range(VX // 2):
            pair = jnp.concatenate([points[2 * m], points[2 * m + 1]], axis=0)
            top = pair.astype(jnp.bfloat16)
            rest = pair - top.astype(jnp.float32)
            at_rows = rows(base, 2 * m, 2 * LEVELS)

            def put(start, value):
                lhs[slot, at_rows, pl.ds(start, 128)] = value

            if last:
                both = jnp.where(lane < PLANE - MAIN, pair, pltpu.roll(rest, 64, 1))
                put(3 * MAIN, both.astype(jnp.bfloat16))
                put(3 * MAIN + 128, top)
            else:
                put(t * 128, top)
                put(MAIN + t * 128, rest.astype(jnp.bfloat16))
                put(2 * MAIN + t * 128, top)

    def prepare_all(slot, which, source):
        for cell in range(cells):
            for t in range(tiles):
                base = cell * per_cell
                prepare(slot, which, source, base, pl.ds(t * 128, 128), t, t == tiles - 1)

    def product(slot, start, width):
        return jnp.dot(
            lhs[slot], back[:, pl.ds(start, width)], preferred_element_type=jnp.float32
        )

    for direction in range(2):
        prepare_all(0, direction, spec)
        prepare_all(1, 2 + direction, mixed)
        for start, width in chunks:
            left[:, pl.ds(start, width)] = product(0, start, width)
        for start, width in chunks:
            cols = pl.ds(start, width)
            value = left[:, cols] * product(1, start, width)
            gain[:, cols] = value if direction == 0 else gain[:, cols] + value
    prepare_all(0, 4, mixed)
    for start, width in chunks:
        loss = product(0, start, width)
        for cell in range(cells):
            at_rows = pl.ds(cell * per_cell, per_cell)
            keep = min(width, PLANE - start)
            fields = g[at_rows, pl.ds(start, width)].astype(jnp.float32)
            part = loss[cell * per_cell : (cell + 1) * per_cell]
            value = fields + weights[cell] * (
                gain[at_rows, pl.ds(start, width)] - fields * part
            )
            out[at_rows, pl.ds(start, keep)] = value[:, :keep].astype(jnp.bfloat16)


def collide(weights, block, bank, coefs, back):
    count = block.shape[1] // 2 * VX * LEVELS
    smem = pl.BlockSpec(memory_space=pltpu.SMEM)
    vmem = pl.BlockSpec(memory_space=pltpu.VMEM)
    return pl.pallas_call(
        collide_kernel,
        out_shape=jax.ShapeDtypeStruct((count, PLANE), jnp.bfloat16),
        in_specs=[smem] + [vmem] * 4,
        out_specs=vmem,
        scratch_shapes=[
            pltpu.VMEM((count, YZ), jnp.bfloat16),
            pltpu.VMEM((count, YZ), jnp.float32),
            pltpu.VMEM((count, YZ), jnp.float32),
            pltpu.VMEM((2, count, DEPTH), jnp.bfloat16),
            pltpu.VMEM((count, YZ), jnp.float32),
            pltpu.VMEM((count, YZ), jnp.float32),
        ],
        compiler_params=pltpu.CompilerParams(vmem_limit_bytes=16 * 1024 * 1024),
        cost_estimate=pl.CostEstimate(
            flops=8_000_000_000, bytes_accessed=8_000_000, transcendentals=0
        ),
    )(weights, block, bank, coefs, back)


def ring(count, step):
    return [(i, (i + step) % count) for i in range(count)]


def body(distribution, wall_mask, pair_table, trans_weight, kernels):
    rows_x, rows_y, local_vx, row_width = distribution.shape
    count_x = lax.axis_size("gx")
    count_y = lax.axis_size("gy")
    count_v = lax.axis_size("vert")
    at_v = lax.axis_index("vert")
    forward = at_v >= count_v // 2

    own = distribution.reshape(rows_x, 2, SUB, LEVELS, 2, HALF)
    own = own.transpose(1, 4, 0, 3, 2, 5).reshape(4, rows_x, LEVELS, LANES)
    own = jnp.pad(own, ((0, 0), (0, 0), (0, 0), (0, WIDE - LANES)))

    low = lax.ppermute(jnp.stack([own[1], own[3], own[2]]), "gy", ring(count_y, 1))
    high_ = lax.ppermute(jnp.stack([own[0], own[2], own[1]]), "gy", ring(count_y, -1))
    openness = open_share(wall_mask)
    wrapped = jnp.pad(openness, 1, mode="wrap")
    anchor_x = lax.axis_index("gx") * rows_x
    anchor_y = lax.axis_index("gy") * rows_y
    window = lax.dynamic_slice(wrapped, (anchor_x, anchor_y), (rows_x + 2, rows_y + 2))
    open_x = window[:, 1 : rows_y + 1]
    face_x = jnp.minimum(open_x[:-1], open_x[1:])
    face_x = jnp.where(forward, face_x, face_x[::-1])
    open_y = window[1 : rows_x + 1]
    face_y = jnp.minimum(open_y[:, :-1], open_y[:, 1:])
    own_x, face_x, face_y = lax.optimization_barrier((own, face_x, face_y))
    upstream = jnp.where(forward, own_x[:, rows_x - 2 :], own_x[:, 1::-1])
    downstream = jnp.where(forward, own_x[:, :1], own_x[:, rows_x - 1 :])
    send_up, send_down = [], []
    for i in range(count_x):
        for v in range(count_v):
            step = 1 if v >= count_v // 2 else -1
            send_up.append((i * count_v + v, (i + step) % count_x * count_v + v))
            send_down.append((i * count_v + v, (i - step) % count_x * count_v + v))
    xup = lax.ppermute(upstream, ("gx", "vert"), send_up)
    xdn = lax.ppermute(downstream, ("gx", "vert"), send_down)

    own_open = lax.dynamic_slice(openness, (anchor_x + at_v, anchor_y), (1, rows_y))[0]

    index_x = at_v * local_vx + jnp.arange(WIDE, dtype=jnp.int32) // HALF
    speeds_x = jnp.abs(speed(index_x.astype(jnp.float32)))
    speeds_x = jnp.broadcast_to(speeds_x[None], (LEVELS, WIDE))
    speeds_y = jnp.asarray(lane_speeds())
    flag = forward.astype(jnp.int32).reshape(1)
    transported = transport(flag, face_x, face_y, own, xup, xdn, low, high_, speeds_x, speeds_y)

    block = lax.all_to_all(transported, "vert", split_axis=0, concat_axis=0, tiled=True)
    entries = jnp.arange(trans_weight.shape[0], dtype=jnp.int32)
    mixing = jnp.sum(
        jnp.where(
            pair_table[:, :, None] == entries[None, None, :], trans_weight[None, None, :], 0.0
        ),
        axis=-1,
    )
    level = np.arange(LEVELS)
    chosen = (level[None, :, None] - level[:, None, None]) % LEVELS == level[None, None, :]
    coefs = jnp.sum(jnp.where(chosen, mixing[None], 0.0), axis=-1)
    coefs = jnp.broadcast_to(coefs[:, :, None], (LEVELS, LEVELS, 128))
    bank = kernels.reshape(kernels.shape[0], VX, PLANE)[:, : VX // 2 + 1]
    twice = np.full((VX // 2 + 1,), 2.0, np.float32)
    twice[0] = twice[VX // 2] = 1.0
    bank = bank * (twice / float(VX * PLANE)).reshape(1, -1, 1)
    bank = jnp.pad(bank, ((0, 0), (0, 0), (0, YZ - PLANE)))
    updated = collide(
        collide_step * own_open, block, bank, coefs, jnp.asarray(split_table())
    )
    updated = updated.reshape(1, 2, VX, row_width)
    return lax.all_to_all(updated, "vert", split_axis=2, concat_axis=0, tiled=True)


def solution(mesh):
    in_specs = (P("gx", "gy", "vert", None), P(), P(), P(), P())
    out_specs = P("gx", "gy", "vert", None)
    return jax.shard_map(body, mesh=mesh, in_specs=in_specs, out_specs=out_specs, check_vma=False)
```

```python
import math

import ml_dtypes
import numpy as np
import jax
import jax.numpy as jnp
from jax import lax
from jax.experimental import pallas as pl
from jax.experimental.pallas import tpu as pltpu
from jax.sharding import PartitionSpec as P

VX = 24
VY = 24
VZ = 24
LEVELS = 8
PLANE = VY * VZ
HALF = PLANE // 2
SUB = 3
LANES = SUB * HALF
WIDE = 896
YZ = 640
MAIN = 512
DEPTH = 3 * MAIN + 256
HIGH_ORDER = (1, 3, 2)
LOW_ORDER = (0, 2, 1)

courant = 0.45
collide_step = 0.4


def open_share(wall_mask):
    return jnp.where(wall_mask == 1, 0.0, jnp.where(wall_mask == 2, 0.5, 1.0)).astype(jnp.float32)


def cas_matrix(extent):
    counter = np.arange(extent)
    angles = (np.outer(counter, counter) % extent) * (2.0 * np.pi / extent)
    return np.cos(angles) + np.sin(angles)


def speed(index):
    return courant * (2.0 * index - (VX - 1)) / (VX - 1)


def lane_speeds():
    rows = []
    for half in range(2):
        j = np.arange(HALF) // VZ + half * (VY // 2)
        row = np.zeros((WIDE,), np.float32)
        row[:LANES] = np.tile(np.abs(speed(j)), SUB)
        rows.append(np.broadcast_to(row, (LEVELS, WIDE)))
    return np.stack(rows).astype(np.float32)


def minmod(a, b):
    return jnp.maximum(jnp.minimum(a, b), jnp.minimum(jnp.maximum(a, b), 0.0))


def split_kernel(flags, raw, own, to_low, to_high, to_down, to_up):
    rows_x = raw.shape[0]
    blank = jnp.zeros((LEVELS, WIDE - LANES), jnp.float32)
    for x in range(rows_x):
        for y in range(2):
            wide = [raw[x, i, y].astype(jnp.float32) for i in range(SUB)]
            for half in range(2):
                q = 2 * y + half
                cut = [part[:, half * HALF : (half + 1) * HALF] for part in wide]
                value = jnp.concatenate(cut + [blank], axis=1).astype(jnp.bfloat16)
                own[q, x] = value
                if q in HIGH_ORDER:
                    to_high[HIGH_ORDER.index(q), x] = value
                if q in LOW_ORDER:
                    to_low[LOW_ORDER.index(q), x] = value
    forward = flags[0] > 0
    for q in range(4):
        for step in range(2):
            row = jnp.where(forward, rows_x - 2 + step, 1 - step)
            to_down[q, step] = own[q, row]
        to_up[q, 0] = own[q, jnp.where(forward, 0, rows_x - 1)]


def split(flag, raw):
    rows_x = raw.shape[0]
    smem = pl.BlockSpec(memory_space=pltpu.SMEM)
    vmem = pl.BlockSpec(memory_space=pltpu.VMEM)
    shapes = [(4, rows_x), (3, rows_x), (3, rows_x), (4, 2), (4, 1)]
    return pl.pallas_call(
        split_kernel,
        out_shape=[jax.ShapeDtypeStruct(shape + (LEVELS, WIDE), jnp.bfloat16) for shape in shapes],
        in_specs=[smem, vmem],
        out_specs=[vmem] * 5,
        compiler_params=pltpu.CompilerParams(vmem_limit_bytes=16 * 1024 * 1024),
        cost_estimate=pl.CostEstimate(flops=1_000_000, bytes_accessed=2_000_000, transcendentals=0),
    )(flag, raw)


def along_x_kernel(flags, face_x, own, xup, xdn, speeds_x, part):
    rows_x = own.shape[1]
    forward = flags[0] > 0

    def pick(step):
        return jnp.where(forward, step, rows_x - 1 - step)

    def tile(t, carry):
        lanes = pl.ds(pl.multiple_of(t * 128, 128), 128)
        nu_x = speeds_x[:, lanes]
        half_x = 0.5 * (1.0 - nu_x)
        for q in range(4):
            y = q // 2
            far = xup[q, 0, :, lanes].astype(jnp.float32)
            near = xup[q, 1, :, lanes].astype(jnp.float32)
            now = own[q, pick(0), :, lanes].astype(jnp.float32)
            diff = now - near
            flux = face_x[0, y] * (nu_x * (near + half_x * minmod(near - far, diff)))
            for step in range(rows_x):
                if step + 1 < rows_x:
                    nxt = own[q, pick(step + 1), :, lanes].astype(jnp.float32)
                else:
                    nxt = xdn[q, 0, :, lanes].astype(jnp.float32)
                later = nxt - now
                flux_out = face_x[step + 1, y] * (nu_x * (now + half_x * minmod(diff, later)))
                part[q, pick(step), :, lanes] = now + (flux - flux_out)
                now, diff, flux = nxt, later, flux_out
        return carry

    lax.fori_loop(0, WIDE // 128, tile, 0)


def along_y_kernel(face_y, part, own, low, high_, speeds_y, out):
    rows_x = own.shape[1]

    def tile(t, carry):
        lanes = pl.ds(pl.multiple_of(t * 128, 128), 128)
        for half in range(2):
            nu_y = speeds_y[half, :, lanes]
            half_y = 0.5 * (1.0 - nu_y)
            first, second = (half, 2 + half) if half == 1 else (2 + half, half)
            w0, w1, w2 = (0, 1, 2) if half == 1 else (2, 1, 0)
            for row in range(rows_x):

                def f32(ref, at):
                    return ref[at, row, :, lanes].astype(jnp.float32)

                if half == 1:
                    up2, up1, down = f32(low, 0), f32(low, 1), f32(high_, 2)
                else:
                    up2, up1, down = f32(high_, 1), f32(high_, 0), f32(low, 2)
                a, b = f32(own, first), f32(own, second)
                d0, d1, d2, d3 = up1 - up2, a - up1, b - a, down - b
                g0 = face_y[row, w0] * (nu_y * (up1 + half_y * minmod(d0, d1)))
                g1 = face_y[row, w1] * (nu_y * (a + half_y * minmod(d1, d2)))
                g2 = face_y[row, w2] * (nu_y * (b + half_y * minmod(d2, d3)))
                for at, change in ((first, g0 - g1), (second, g1 - g2)):
                    value = part[at, row, :, lanes] + change
                    out[row, at, :, lanes] = value.astype(jnp.bfloat16)
        return carry

    lax.fori_loop(0, WIDE // 128, tile, 0)


def along_x(flag, face_x, own, xup, xdn, speeds_x):
    smem = pl.BlockSpec(memory_space=pltpu.SMEM)
    vmem = pl.BlockSpec(memory_space=pltpu.VMEM)
    return pl.pallas_call(
        along_x_kernel,
        out_shape=jax.ShapeDtypeStruct(own.shape, jnp.float32),
        in_specs=[smem] * 2 + [vmem] * 4,
        out_specs=vmem,
        compiler_params=pltpu.CompilerParams(vmem_limit_bytes=16 * 1024 * 1024),
        cost_estimate=pl.CostEstimate(flops=5_000_000, bytes_accessed=1_500_000, transcendentals=0),
    )(flag, face_x, own, xup, xdn, speeds_x)


def along_y(face_y, part, own, low, high_, speeds_y):
    rows_x = own.shape[1]
    smem = pl.BlockSpec(memory_space=pltpu.SMEM)
    vmem = pl.BlockSpec(memory_space=pltpu.VMEM)
    return pl.pallas_call(
        along_y_kernel,
        out_shape=jax.ShapeDtypeStruct((rows_x, 4, LEVELS, WIDE), jnp.bfloat16),
        in_specs=[smem] + [vmem] * 5,
        out_specs=vmem,
        compiler_params=pltpu.CompilerParams(vmem_limit_bytes=16 * 1024 * 1024),
        cost_estimate=pl.CostEstimate(flops=5_000_000, bytes_accessed=2_500_000, transcendentals=0),
    )(face_y, part, own, low, high_, speeds_y)


def small(matrix, inputs):
    products = {}

    def product(scale, n):
        if scale == 1.0:
            return inputs[n]
        if (scale, n) not in products:
            products[scale, n] = inputs[n] * scale
        return products[scale, n]

    results = []
    for row in matrix:
        total = None
        for n, value in enumerate(row):
            value = round(float(value), 12)
            if value == 0.0:
                continue
            term = product(abs(value), n)
            if total is None:
                total = term if value > 0 else -term
            else:
                total = total + term if value > 0 else total - term
        results.append(total)
    return results


def trig(function, outs, ins, over):
    return [[function(math.pi * k * n / over) for n in ins] for k in outs]


def cosines(v):
    e = [v[n] + v[12 - n] for n in range(6)] + [v[6]]
    o = [v[n] - v[12 - n] for n in range(6)]
    ee = [e[n] + e[6 - n] for n in range(3)] + [e[3]]
    eo = [e[n] - e[6 - n] for n in range(3)]
    out = [None] * 13
    out[0::4] = small(trig(math.cos, range(4), range(4), 3), ee)
    out[2::4] = small(trig(math.cos, (1, 3, 5), range(3), 6), eo)
    out[1::2] = small(trig(math.cos, (1, 3, 5, 7, 9, 11), range(6), 12), o)
    return out


def sines(v):
    v = [None] + v
    f = [v[n] + v[12 - n] for n in range(1, 6)] + [v[6]]
    g = [None] + [v[n] - v[12 - n] for n in range(1, 6)]
    gp = [g[1] + g[5], g[2] + g[4], g[3]]
    gm = [g[1] - g[5], g[2] - g[4]]
    out = [None] * 11
    out[0::2] = small(trig(math.sin, (1, 3, 5, 7, 9, 11), range(1, 7), 12), f)
    out[1::4] = small(trig(math.sin, (1, 3, 5), (1, 2, 3), 6), gp)
    out[3::4] = small(trig(math.sin, (2, 4), (1, 2), 6), gm)
    return out


def modes_of(x):
    even = [x[0]] + [x[n] + x[VX - n] for n in range(1, 12)] + [x[12]]
    odd = [x[n] - x[VX - n] for n in range(1, 12)]
    return cosines(even) + sines(odd)


def points_of(modes):
    p = cosines(modes[:13])
    q = sines(modes[13:])
    out = [None] * VX
    out[0], out[12] = p[0], p[12]
    for n in range(1, 12):
        out[n] = p[n] + q[n - 1]
        out[VX - n] = p[n] - q[n - 1]
    return out


def split_table():
    table = np.kron(cas_matrix(VY), cas_matrix(VZ)).astype(np.float32)
    table = np.pad(table, ((0, 0), (0, YZ - PLANE)))
    top = table.astype(ml_dtypes.bfloat16)
    low = (table - top.astype(np.float32)).astype(ml_dtypes.bfloat16)
    rest = PLANE - MAIN
    back = np.zeros((DEPTH, YZ), ml_dtypes.bfloat16)
    back[0:MAIN] = top[:MAIN]
    back[MAIN : 2 * MAIN] = top[:MAIN]
    back[2 * MAIN : 3 * MAIN] = low[:MAIN]
    back[3 * MAIN : 3 * MAIN + rest] = top[MAIN:PLANE]
    back[3 * MAIN + rest : 3 * MAIN + 2 * rest] = top[MAIN:PLANE]
    back[3 * MAIN + 128 : 3 * MAIN + 128 + rest] = low[MAIN:PLANE]
    return back


def collide_kernel(
    weights, block, bank, coefs, back, out, g, spec, mixed, lhs, left, gain
):
    cells = block.shape[1] // 2
    per_cell = VX * LEVELS
    blank = jnp.zeros((LEVELS, YZ - PLANE), jnp.float32)

    def plane(cell, a):
        source, i = a // SUB, a % SUB
        wide = [block[source, 2 * cell + half].astype(jnp.float32) for half in range(2)]
        cut = [part[:, i * HALF : (i + 1) * HALF] for part in wide]
        return jnp.concatenate(cut + [blank], axis=1)

    for cell in range(cells):
        for m in range(VX // 2):
            pair = jnp.concatenate([plane(cell, 2 * m), plane(cell, 2 * m + 1)], axis=0)
            at_rows = pl.ds(cell * per_cell + 2 * m * LEVELS, 2 * LEVELS)
            g[at_rows, :] = pair.astype(jnp.bfloat16)

    tiles = YZ // 128
    chunks = ((0, 256), (256, 256), (512, 128))

    edge = jnp.concatenate([g[:, MAIN:], g[:, MAIN:]], axis=1)
    for start, width in chunks:
        cols = pl.ds(start, width)
        total = jnp.dot(edge, back[3 * MAIN :, cols], preferred_element_type=jnp.float32)
        for first in (0, 2 * MAIN):
            total = total + jnp.dot(
                g[:, :MAIN], back[pl.ds(first, MAIN), cols], preferred_element_type=jnp.float32
            )
        spec[:, cols] = total

    def rows(base, a, count=LEVELS):
        return pl.ds(base + a * LEVELS, count)

    def ahead(index):
        base, lanes = index // tiles * per_cell, pl.ds(index % tiles * 128, 128)
        modes = modes_of([spec[rows(base, a), lanes] for a in range(VX)])
        for a in range(VX):
            total = coefs[0] * modes[a]
            for shift in range(1, LEVELS):
                total = total + coefs[shift] * pltpu.roll(modes[a], shift, 0)
            spec[rows(base, a), lanes] = modes[a]
            mixed[rows(base, a), lanes] = total

    for index in range(cells * tiles):
        ahead(index)

    lane = lax.broadcasted_iota(jnp.int32, (2 * LEVELS, 128), 1)

    def prepare(slot, which, source, base, lanes, t, last):
        factors = [bank[which, pl.ds(k, 1), lanes] for k in range(13)]
        points = points_of(
            [source[rows(base, a), lanes] * factors[a if a < 13 else a - 12] for a in range(VX)]
        )
        for m in range(VX // 2):
            pair = jnp.concatenate([points[2 * m], points[2 * m + 1]], axis=0)
            top = pair.astype(jnp.bfloat16)
            rest = pair - top.astype(jnp.float32)
            at_rows = rows(base, 2 * m, 2 * LEVELS)

            def put(start, value):
                lhs[slot, at_rows, pl.ds(start, 128)] = value

            if last:
                both = jnp.where(lane < PLANE - MAIN, pair, pltpu.roll(rest, 64, 1))
                put(3 * MAIN, both.astype(jnp.bfloat16))
                put(3 * MAIN + 128, top)
            else:
                put(t * 128, top)
                put(MAIN + t * 128, rest.astype(jnp.bfloat16))
                put(2 * MAIN + t * 128, top)

    def prepare_all(slot, which, source):
        for cell in range(cells):
            for t in range(tiles):
                base = cell * per_cell
                prepare(slot, which, source, base, pl.ds(t * 128, 128), t, t == tiles - 1)

    def product(slot, start, width):
        return jnp.dot(
            lhs[slot], back[:, pl.ds(start, width)], preferred_element_type=jnp.float32
        )

    for direction in range(2):
        prepare_all(2 * direction, direction, spec)
        prepare_all(2 * direction + 1, 2 + direction, mixed)
        for start, width in chunks:
            left[:, pl.ds(start, width)] = product(2 * direction, start, width)
        for start, width in chunks:
            cols = pl.ds(start, width)
            value = left[:, cols] * product(2 * direction + 1, start, width)
            gain[:, cols] = value if direction == 0 else gain[:, cols] + value
    prepare_all(4, 4, mixed)
    for start, width in chunks:
        loss = product(4, start, width)
        for cell in range(cells):
            at_rows = pl.ds(cell * per_cell, per_cell)
            keep = min(width, PLANE - start)
            fields = g[at_rows, pl.ds(start, width)].astype(jnp.float32)
            part = loss[cell * per_cell : (cell + 1) * per_cell]
            value = fields + weights[cell] * (
                gain[at_rows, pl.ds(start, width)] - fields * part
            )
            out[at_rows, pl.ds(start, keep)] = value[:, :keep].astype(jnp.bfloat16)


def collide(weights, block, bank, coefs, back):
    count = block.shape[1] // 2 * VX * LEVELS
    smem = pl.BlockSpec(memory_space=pltpu.SMEM)
    vmem = pl.BlockSpec(memory_space=pltpu.VMEM)
    return pl.pallas_call(
        collide_kernel,
        out_shape=jax.ShapeDtypeStruct((count, PLANE), jnp.bfloat16),
        in_specs=[smem] + [vmem] * 4,
        out_specs=vmem,
        scratch_shapes=[
            pltpu.VMEM((count, YZ), jnp.bfloat16),
            pltpu.VMEM((count, YZ), jnp.float32),
            pltpu.VMEM((count, YZ), jnp.float32),
            pltpu.VMEM((5, count, DEPTH), jnp.bfloat16),
            pltpu.VMEM((count, YZ), jnp.float32),
            pltpu.VMEM((count, YZ), jnp.float32),
        ],
        compiler_params=pltpu.CompilerParams(vmem_limit_bytes=16 * 1024 * 1024),
        cost_estimate=pl.CostEstimate(
            flops=8_000_000_000, bytes_accessed=8_000_000, transcendentals=0
        ),
    )(weights, block, bank, coefs, back)


def ring(count, step):
    return [(i, (i + step) % count) for i in range(count)]


def body(distribution, wall_mask, pair_table, trans_weight, kernels):
    rows_x, rows_y, local_vx, row_width = distribution.shape
    count_x = lax.axis_size("gx")
    count_y = lax.axis_size("gy")
    count_v = lax.axis_size("vert")
    at_v = lax.axis_index("vert")
    forward = at_v >= count_v // 2

    flag = forward.astype(jnp.int32).reshape(1)
    raw = distribution.transpose(0, 2, 1, 3).reshape(rows_x, SUB, 2, LEVELS, PLANE)
    own, to_low, to_high, upstream, downstream = split(flag, raw)
    low = lax.ppermute(to_high, "gy", ring(count_y, 1))
    high_ = lax.ppermute(to_low, "gy", ring(count_y, -1))

    openness = open_share(wall_mask)
    wrapped = jnp.pad(openness, 1, mode="wrap")
    anchor_x = lax.axis_index("gx") * rows_x
    anchor_y = lax.axis_index("gy") * rows_y
    window = lax.dynamic_slice(wrapped, (anchor_x, anchor_y), (rows_x + 2, rows_y + 2))
    open_x = window[:, 1 : rows_y + 1]
    face_x = jnp.minimum(open_x[:-1], open_x[1:])
    face_x = jnp.where(forward, face_x, face_x[::-1])
    open_y = window[1 : rows_x + 1]
    face_y = jnp.minimum(open_y[:, :-1], open_y[:, 1:])
    upstream, downstream, face_x, face_y = lax.optimization_barrier(
        (upstream, downstream, face_x, face_y)
    )
    send_up, send_down = [], []
    for i in range(count_x):
        for v in range(count_v):
            step = 1 if v >= count_v // 2 else -1
            send_up.append((i * count_v + v, (i + step) % count_x * count_v + v))
            send_down.append((i * count_v + v, (i - step) % count_x * count_v + v))
    xup = lax.ppermute(upstream, ("gx", "vert"), send_up)
    xdn = lax.ppermute(downstream, ("gx", "vert"), send_down)

    own_open = lax.dynamic_slice(openness, (anchor_x + at_v, anchor_y), (1, rows_y))[0]

    index_x = at_v * local_vx + jnp.arange(WIDE, dtype=jnp.int32) // HALF
    speeds_x = jnp.abs(speed(index_x.astype(jnp.float32)))
    speeds_x = jnp.broadcast_to(speeds_x[None], (LEVELS, WIDE))
    speeds_y = jnp.asarray(lane_speeds())
    part = along_x(flag, face_x, own, xup, xdn, speeds_x)
    transported = along_y(face_y, part, own, low, high_, speeds_y)

    block = lax.all_to_all(transported, "vert", split_axis=0, concat_axis=0, tiled=True)
    entries = jnp.arange(trans_weight.shape[0], dtype=jnp.int32)
    mixing = jnp.sum(
        jnp.where(
            pair_table[:, :, None] == entries[None, None, :], trans_weight[None, None, :], 0.0
        ),
        axis=-1,
    )
    level = np.arange(LEVELS)
    chosen = (level[None, :, None] - level[:, None, None]) % LEVELS == level[None, None, :]
    coefs = jnp.sum(jnp.where(chosen, mixing[None], 0.0), axis=-1)
    coefs = jnp.broadcast_to(coefs[:, :, None], (LEVELS, LEVELS, 128))
    bank = kernels.reshape(kernels.shape[0], VX, PLANE)[:, : VX // 2 + 1]
    twice = np.full((VX // 2 + 1,), 2.0, np.float32)
    twice[0] = twice[VX // 2] = 1.0
    bank = bank * (twice / float(VX * PLANE)).reshape(1, -1, 1)
    bank = jnp.pad(bank, ((0, 0), (0, 0), (0, YZ - PLANE)))
    updated = collide(
        collide_step * own_open, block, bank, coefs, jnp.asarray(split_table())
    )
    updated = updated.reshape(1, 2, VX, row_width)
    return lax.all_to_all(updated, "vert", split_axis=2, concat_axis=0, tiled=True)


def solution(mesh):
    in_specs = (P("gx", "gy", "vert", None), P(), P(), P(), P())
    out_specs = P("gx", "gy", "vert", None)
    return jax.shard_map(body, mesh=mesh, in_specs=in_specs, out_specs=out_specs, check_vma=False)
```

```python
import math

import ml_dtypes
import numpy as np
import jax
import jax.numpy as jnp
from jax import lax
from jax.experimental import pallas as pl
from jax.experimental.pallas import tpu as pltpu
from jax.sharding import PartitionSpec as P

NX = 64
NY = 16
VX = 24
VY = 24
VZ = 24
LEVELS = 8
PLANE = VY * VZ
HALF = PLANE // 2
SUB = 3
LANES = SUB * HALF
WIDE = 896
YZ = 640
MAIN = 512
DEPTH = 2 * MAIN + 256
HIGH_ORDER = (1, 3, 2)
LOW_ORDER = (0, 2, 1)

courant = 0.45
collide_step = 0.4


def open_share(wall_mask):
    return jnp.where(wall_mask == 1, 0.0, jnp.where(wall_mask == 2, 0.5, 1.0)).astype(jnp.float32)


def cas_matrix(extent):
    counter = np.arange(extent)
    angles = (np.outer(counter, counter) % extent) * (2.0 * np.pi / extent)
    return np.cos(angles) + np.sin(angles)


def speed(index):
    return courant * (2.0 * index - (VX - 1)) / (VX - 1)


def lane_speeds():
    rows = []
    for half in range(2):
        j = np.arange(HALF) // VZ + half * (VY // 2)
        row = np.zeros((WIDE,), np.float32)
        row[:LANES] = np.tile(np.abs(speed(j)), SUB)
        rows.append(np.broadcast_to(row, (LEVELS, WIDE)))
    return np.stack(rows).astype(np.float32)


def minmod(a, b):
    return jnp.maximum(jnp.minimum(a, b), jnp.minimum(jnp.maximum(a, b), 0.0))


def split_kernel(raw, own, to_low, to_high):
    rows_x = raw.shape[0]
    blank = jnp.zeros((LEVELS, WIDE - LANES), jnp.float32)
    for x in range(rows_x):
        for y in range(2):
            wide = [raw[x, i, y].astype(jnp.float32) for i in range(SUB)]
            for half in range(2):
                q = 2 * y + half
                cut = [part[:, half * HALF : (half + 1) * HALF] for part in wide]
                value = jnp.concatenate(cut + [blank], axis=1).astype(jnp.bfloat16)
                own[q, x] = value
                if q in HIGH_ORDER:
                    to_high[HIGH_ORDER.index(q), x] = value
                if q in LOW_ORDER:
                    to_low[LOW_ORDER.index(q), x] = value


def edges_kernel(flags, own, to_down, to_up):
    rows_x = own.shape[1]
    forward = flags[0] > 0
    for q in range(4):
        for step in range(2):
            row = jnp.where(forward, rows_x - 2 + step, 1 - step)
            to_down[q, step] = own[q, row]
        to_up[q, 0] = own[q, jnp.where(forward, 0, rows_x - 1)]


def edges(flag, own):
    smem = pl.BlockSpec(memory_space=pltpu.SMEM)
    vmem = pl.BlockSpec(memory_space=pltpu.VMEM)
    return pl.pallas_call(
        edges_kernel,
        out_shape=[
            jax.ShapeDtypeStruct((4, count, LEVELS, WIDE), jnp.bfloat16) for count in (2, 1)
        ],
        in_specs=[smem, vmem],
        out_specs=[vmem] * 2,
        compiler_params=pltpu.CompilerParams(vmem_limit_bytes=8 * 1024 * 1024),
        cost_estimate=pl.CostEstimate(flops=100_000, bytes_accessed=400_000, transcendentals=0),
    )(flag, own)


def split(raw):
    rows_x = raw.shape[0]
    vmem = pl.BlockSpec(memory_space=pltpu.VMEM)
    shapes = [(4, rows_x), (3, rows_x), (3, rows_x)]
    return pl.pallas_call(
        split_kernel,
        out_shape=[jax.ShapeDtypeStruct(shape + (LEVELS, WIDE), jnp.bfloat16) for shape in shapes],
        in_specs=[vmem],
        out_specs=[vmem] * 3,
        compiler_params=pltpu.CompilerParams(vmem_limit_bytes=8 * 1024 * 1024),
        cost_estimate=pl.CostEstimate(flops=1_000_000, bytes_accessed=2_000_000, transcendentals=0),
    )(raw)


def open_at(mask, row, column):
    flag = mask[lax.rem(row + NX, NX), lax.rem(column + NY, NY)]
    return jnp.where(flag == 1, 0.0, jnp.where(flag == 2, 0.5, 1.0)).astype(jnp.float32)


def along_x_kernel(flags, mask, own, xup, xdn, speeds_x, part, face_x):
    rows_x = own.shape[1]
    forward = flags[0] > 0

    def pick(step):
        return jnp.where(forward, step, rows_x - 1 - step)

    for y in range(2):
        cells = [open_at(mask, flags[1] + pick(step), flags[2] + y) for step in range(-1, rows_x + 1)]
        for step in range(rows_x + 1):
            face_x[step, y] = jnp.minimum(cells[step], cells[step + 1])

    def tile(t, carry):
        lanes = pl.ds(pl.multiple_of(t * 128, 128), 128)
        nu_x = speeds_x[:, lanes]
        half_x = 0.5 * (1.0 - nu_x)
        for q in range(4):
            y = q // 2
            far = xup[q, 0, :, lanes].astype(jnp.float32)
            near = xup[q, 1, :, lanes].astype(jnp.float32)
            now = own[q, pick(0), :, lanes].astype(jnp.float32)
            diff = now - near
            flux = face_x[0, y] * (nu_x * (near + half_x * minmod(near - far, diff)))
            for step in range(rows_x):
                if step + 1 < rows_x:
                    nxt = own[q, pick(step + 1), :, lanes].astype(jnp.float32)
                else:
                    nxt = xdn[q, 0, :, lanes].astype(jnp.float32)
                later = nxt - now
                flux_out = face_x[step + 1, y] * (nu_x * (now + half_x * minmod(diff, later)))
                part[q, pick(step), :, lanes] = now + (flux - flux_out)
                now, diff, flux = nxt, later, flux_out
        return carry

    lax.fori_loop(0, WIDE // 128, tile, 0)


def along_y_kernel(flags, mask, part, own, low, high_, speeds_y, out, face_y):
    rows_x = own.shape[1]
    for row in range(rows_x):
        cells = [open_at(mask, flags[1] + row, flags[2] + y) for y in range(-1, 3)]
        for face in range(3):
            face_y[row, face] = jnp.minimum(cells[face], cells[face + 1])

    def tile(t, carry):
        lanes = pl.ds(pl.multiple_of(t * 128, 128), 128)
        for half in range(2):
            nu_y = speeds_y[half, :, lanes]
            half_y = 0.5 * (1.0 - nu_y)
            first, second = (half, 2 + half) if half == 1 else (2 + half, half)
            w0, w1, w2 = (0, 1, 2) if half == 1 else (2, 1, 0)
            for row in range(rows_x):

                def f32(ref, at):
                    return ref[at, row, :, lanes].astype(jnp.float32)

                if half == 1:
                    up2, up1, down = f32(low, 0), f32(low, 1), f32(high_, 2)
                else:
                    up2, up1, down = f32(high_, 1), f32(high_, 0), f32(low, 2)
                a, b = f32(own, first), f32(own, second)
                d0, d1, d2, d3 = up1 - up2, a - up1, b - a, down - b
                g0 = face_y[row, w0] * (nu_y * (up1 + half_y * minmod(d0, d1)))
                g1 = face_y[row, w1] * (nu_y * (a + half_y * minmod(d1, d2)))
                g2 = face_y[row, w2] * (nu_y * (b + half_y * minmod(d2, d3)))
                for at, change in ((first, g0 - g1), (second, g1 - g2)):
                    value = part[at, row, :, lanes] + change
                    out[row, at, :, lanes] = value.astype(jnp.bfloat16)
        return carry

    lax.fori_loop(0, WIDE // 128, tile, 0)


def along_x(flag, mask, own, xup, xdn, speeds_x):
    smem = pl.BlockSpec(memory_space=pltpu.SMEM)
    vmem = pl.BlockSpec(memory_space=pltpu.VMEM)
    return pl.pallas_call(
        along_x_kernel,
        out_shape=jax.ShapeDtypeStruct(own.shape, jnp.float32),
        in_specs=[smem] * 2 + [vmem] * 4,
        out_specs=vmem,
        scratch_shapes=[pltpu.SMEM((own.shape[1] + 1, 2), jnp.float32)],
        compiler_params=pltpu.CompilerParams(vmem_limit_bytes=8 * 1024 * 1024),
        cost_estimate=pl.CostEstimate(flops=5_000_000, bytes_accessed=1_500_000, transcendentals=0),
    )(flag, mask, own, xup, xdn, speeds_x)


def along_y(flag, mask, part, own, low, high_, speeds_y):
    rows_x = own.shape[1]
    smem = pl.BlockSpec(memory_space=pltpu.SMEM)
    vmem = pl.BlockSpec(memory_space=pltpu.VMEM)
    return pl.pallas_call(
        along_y_kernel,
        out_shape=jax.ShapeDtypeStruct((rows_x, 4, LEVELS, WIDE), jnp.bfloat16),
        in_specs=[smem] * 2 + [vmem] * 5,
        out_specs=vmem,
        scratch_shapes=[pltpu.SMEM((rows_x, 3), jnp.float32)],
        compiler_params=pltpu.CompilerParams(vmem_limit_bytes=8 * 1024 * 1024),
        cost_estimate=pl.CostEstimate(flops=5_000_000, bytes_accessed=2_500_000, transcendentals=0),
    )(flag, mask, part, own, low, high_, speeds_y)


def small(matrix, inputs):
    products = {}

    def product(scale, n):
        if scale == 1.0:
            return inputs[n]
        if (scale, n) not in products:
            products[scale, n] = inputs[n] * scale
        return products[scale, n]

    results = []
    for row in matrix:
        total = None
        for n, value in enumerate(row):
            value = round(float(value), 12)
            if value == 0.0:
                continue
            term = product(abs(value), n)
            if total is None:
                total = term if value > 0 else -term
            else:
                total = total + term if value > 0 else total - term
        results.append(total)
    return results


def trig(function, outs, ins, over):
    return [[function(math.pi * k * n / over) for n in ins] for k in outs]


def cosines(v):
    e = [v[n] + v[12 - n] for n in range(6)] + [v[6]]
    o = [v[n] - v[12 - n] for n in range(6)]
    ee = [e[n] + e[6 - n] for n in range(3)] + [e[3]]
    eo = [e[n] - e[6 - n] for n in range(3)]
    out = [None] * 13
    out[0::4] = small(trig(math.cos, range(4), range(4), 3), ee)
    out[2::4] = small(trig(math.cos, (1, 3, 5), range(3), 6), eo)
    out[1::2] = small(trig(math.cos, (1, 3, 5, 7, 9, 11), range(6), 12), o)
    return out


def sines(v):
    v = [None] + v
    f = [v[n] + v[12 - n] for n in range(1, 6)] + [v[6]]
    g = [None] + [v[n] - v[12 - n] for n in range(1, 6)]
    gp = [g[1] + g[5], g[2] + g[4], g[3]]
    gm = [g[1] - g[5], g[2] - g[4]]
    out = [None] * 11
    out[0::2] = small(trig(math.sin, (1, 3, 5, 7, 9, 11), range(1, 7), 12), f)
    out[1::4] = small(trig(math.sin, (1, 3, 5), (1, 2, 3), 6), gp)
    out[3::4] = small(trig(math.sin, (2, 4), (1, 2), 6), gm)
    return out


def modes_of(x):
    even = [x[0]] + [x[n] + x[VX - n] for n in range(1, 12)] + [x[12]]
    odd = [x[n] - x[VX - n] for n in range(1, 12)]
    return cosines(even) + sines(odd)


def points_of(modes):
    p = cosines(modes[:13])
    q = sines(modes[13:])
    out = [None] * VX
    out[0], out[12] = p[0], p[12]
    for n in range(1, 12):
        out[n] = p[n] + q[n - 1]
        out[VX - n] = p[n] - q[n - 1]
    return out


def split_table():
    table = np.kron(cas_matrix(VY), cas_matrix(VZ)).astype(np.float32)
    table = np.pad(table, ((0, 0), (0, YZ - PLANE)))
    top = table.astype(ml_dtypes.bfloat16)
    low = (table - top.astype(np.float32)).astype(ml_dtypes.bfloat16)
    rest = PLANE - MAIN
    back = np.zeros((DEPTH, YZ), ml_dtypes.bfloat16)
    back[0:MAIN] = top[:MAIN]
    back[MAIN : 2 * MAIN] = low[:MAIN]
    back[2 * MAIN : 2 * MAIN + rest] = top[MAIN:PLANE]
    back[2 * MAIN + rest : 2 * MAIN + 2 * rest] = top[MAIN:PLANE]
    back[2 * MAIN + 128 : 2 * MAIN + 128 + rest] = low[MAIN:PLANE]
    return back


def collide_kernel(
    weights, block, bank, coefs, back, out, g, spec, mixed, lhs, left, gain
):
    cells = block.shape[1] // 2
    per_cell = VX * LEVELS
    blank = jnp.zeros((LEVELS, YZ - PLANE), jnp.float32)

    def plane(cell, a):
        source, i = a // SUB, a % SUB
        wide = [block[source, 2 * cell + half].astype(jnp.float32) for half in range(2)]
        cut = [part[:, i * HALF : (i + 1) * HALF] for part in wide]
        return jnp.concatenate(cut + [blank], axis=1)

    for cell in range(cells):
        for m in range(VX // 2):
            pair = jnp.concatenate([plane(cell, 2 * m), plane(cell, 2 * m + 1)], axis=0)
            at_rows = pl.ds(cell * per_cell + 2 * m * LEVELS, 2 * LEVELS)
            g[at_rows, :] = pair.astype(jnp.bfloat16)

    tiles = YZ // 128
    chunks = ((0, 256), (256, 256), (512, 128))

    edge = jnp.concatenate([g[:, MAIN:], g[:, MAIN:]], axis=1)
    for start, width in chunks:
        cols = pl.ds(start, width)
        total = jnp.dot(edge, back[2 * MAIN :, cols], preferred_element_type=jnp.float32)
        for first in (0, MAIN):
            total = total + jnp.dot(
                g[:, :MAIN], back[pl.ds(first, MAIN), cols], preferred_element_type=jnp.float32
            )
        spec[:, cols] = total

    def rows(base, a, count=LEVELS):
        return pl.ds(base + a * LEVELS, count)

    factor = [
        jnp.broadcast_to(coefs[:, shift : shift + 1], (LEVELS, 128)) for shift in range(LEVELS)
    ]

    def ahead(index):
        base, lanes = index // tiles * per_cell, pl.ds(index % tiles * 128, 128)
        modes = modes_of([spec[rows(base, a), lanes] for a in range(VX)])
        for a in range(VX):
            total = factor[0] * modes[a]
            for shift in range(1, LEVELS):
                total = total + factor[shift] * pltpu.roll(modes[a], shift, 0)
            spec[rows(base, a), lanes] = modes[a]
            mixed[rows(base, a), lanes] = total

    for index in range(cells * tiles):
        ahead(index)

    lane = lax.broadcasted_iota(jnp.int32, (2 * LEVELS, 128), 1)

    def prepare(slot, which, source, base, lanes, t, last):
        factors = [bank[which, pl.ds(k, 1), lanes] for k in range(13)]
        points = points_of(
            [source[rows(base, a), lanes] * factors[a if a < 13 else a - 12] for a in range(VX)]
        )
        for m in range(VX // 2):
            pair = jnp.concatenate([points[2 * m], points[2 * m + 1]], axis=0)
            top = pair.astype(jnp.bfloat16)
            rest = pair - top.astype(jnp.float32)
            at_rows = rows(base, 2 * m, 2 * LEVELS)

            def put(start, value):
                lhs[slot, at_rows, pl.ds(start, 128)] = value

            if last:
                both = jnp.where(lane < PLANE - MAIN, pair, pltpu.roll(rest, 64, 1))
                put(2 * MAIN, both.astype(jnp.bfloat16))
                put(2 * MAIN + 128, top)
            else:
                put(t * 128, rest.astype(jnp.bfloat16))
                put(MAIN + t * 128, top)

    def prepare_all(slot, which, source):
        for cell in range(cells):
            for t in range(tiles):
                base = cell * per_cell
                prepare(slot, which, source, base, pl.ds(t * 128, 128), t, t == tiles - 1)

    def product(slot, start, width):
        cols = pl.ds(start, width)
        total = jnp.dot(
            lhs[slot, :, MAIN:], back[MAIN:, cols], preferred_element_type=jnp.float32
        )
        for first in (0, MAIN):
            total = total + jnp.dot(
                lhs[slot, :, pl.ds(first, MAIN)],
                back[:MAIN, cols],
                preferred_element_type=jnp.float32,
            )
        return total

    for direction in range(2):
        prepare_all(2 * direction, direction, spec)
        prepare_all(2 * direction + 1, 2 + direction, mixed)
        for start, width in chunks:
            left[:, pl.ds(start, width)] = product(2 * direction, start, width)
        for start, width in chunks:
            cols = pl.ds(start, width)
            value = left[:, cols] * product(2 * direction + 1, start, width)
            gain[:, cols] = value if direction == 0 else gain[:, cols] + value
    prepare_all(4, 4, mixed)
    for start, width in chunks:
        loss = product(4, start, width)
        for cell in range(cells):
            at_rows = pl.ds(cell * per_cell, per_cell)
            keep = min(width, PLANE - start)
            fields = g[at_rows, pl.ds(start, width)].astype(jnp.float32)
            part = loss[cell * per_cell : (cell + 1) * per_cell]
            value = fields + weights[cell] * (
                gain[at_rows, pl.ds(start, width)] - fields * part
            )
            out[at_rows, pl.ds(start, keep)] = value[:, :keep].astype(jnp.bfloat16)


def resident_kernel(source, out, sem):
    copy = pltpu.make_async_copy(source, out, sem)
    copy.start()
    copy.wait()


def resident(table):
    return pl.pallas_call(
        resident_kernel,
        out_shape=jax.ShapeDtypeStruct(table.shape, table.dtype),
        in_specs=[pl.BlockSpec(memory_space=pl.ANY)],
        out_specs=pl.BlockSpec(memory_space=pltpu.VMEM),
        scratch_shapes=[pltpu.SemaphoreType.DMA],
        compiler_params=pltpu.CompilerParams(vmem_limit_bytes=8 * 1024 * 1024),
        cost_estimate=pl.CostEstimate(flops=0, bytes_accessed=4_600_000, transcendentals=0),
    )(table)


def collide(weights, block, bank, coefs, back):
    count = block.shape[1] // 2 * VX * LEVELS
    smem = pl.BlockSpec(memory_space=pltpu.SMEM)
    vmem = pl.BlockSpec(memory_space=pltpu.VMEM)
    return pl.pallas_call(
        collide_kernel,
        out_shape=jax.ShapeDtypeStruct((count, PLANE), jnp.bfloat16),
        in_specs=[smem] + [vmem] * 4,
        out_specs=vmem,
        scratch_shapes=[
            pltpu.VMEM((count, YZ), jnp.bfloat16),
            pltpu.VMEM((count, YZ), jnp.float32),
            pltpu.VMEM((count, YZ), jnp.float32),
            pltpu.VMEM((5, count, DEPTH), jnp.bfloat16),
            pltpu.VMEM((count, YZ), jnp.float32),
            pltpu.VMEM((count, YZ), jnp.float32),
        ],
        compiler_params=pltpu.CompilerParams(vmem_limit_bytes=16 * 1024 * 1024),
        cost_estimate=pl.CostEstimate(
            flops=8_000_000_000, bytes_accessed=8_000_000, transcendentals=0
        ),
    )(weights, block, bank, coefs, back)


def ring(count, step):
    return [(i, (i + step) % count) for i in range(count)]


def body(distribution, wall_mask, pair_table, trans_weight, kernels):
    rows_x, rows_y, local_vx, row_width = distribution.shape
    count_x = lax.axis_size("gx")
    count_y = lax.axis_size("gy")
    count_v = lax.axis_size("vert")
    at_v = lax.axis_index("vert")
    forward = at_v >= count_v // 2

    anchor_x = lax.axis_index("gx") * rows_x
    anchor_y = lax.axis_index("gy") * rows_y
    flag = jnp.stack([forward.astype(jnp.int32), anchor_x, anchor_y])
    raw = distribution.transpose(0, 2, 1, 3).reshape(rows_x, SUB, 2, LEVELS, PLANE)
    own, to_low, to_high = split(raw)
    low = lax.ppermute(to_high, "gy", ring(count_y, 1))
    high_ = lax.ppermute(to_low, "gy", ring(count_y, -1))

    index_x = at_v * local_vx + jnp.arange(WIDE, dtype=jnp.int32) // HALF
    speeds_x = jnp.abs(speed(index_x.astype(jnp.float32)))
    upstream, downstream = edges(flag, own)
    send_up, send_down = [], []
    for i in range(count_x):
        for v in range(count_v):
            step = 1 if v >= count_v // 2 else -1
            send_up.append((i * count_v + v, (i + step) % count_x * count_v + v))
            send_down.append((i * count_v + v, (i - step) % count_x * count_v + v))
    xup = lax.ppermute(upstream, ("gx", "vert"), send_up)
    xdn = lax.ppermute(downstream, ("gx", "vert"), send_down)

    openness = open_share(wall_mask)
    own_open = lax.dynamic_slice(openness, (anchor_x + at_v, anchor_y), (1, rows_y))[0]

    speeds_x = jnp.broadcast_to(speeds_x[None], (LEVELS, WIDE))
    speeds_y = jnp.asarray(lane_speeds())
    part = along_x(flag, wall_mask, own, xup, xdn, speeds_x)
    transported = along_y(flag, wall_mask, part, own, low, high_, speeds_y)

    back = jnp.asarray(split_table())
    block = lax.all_to_all(transported, "vert", split_axis=0, concat_axis=0, tiled=True)
    entries = jnp.arange(trans_weight.shape[0], dtype=jnp.int32)
    mixing = jnp.sum(
        jnp.where(
            pair_table[:, :, None] == entries[None, None, :], trans_weight[None, None, :], 0.0
        ),
        axis=-1,
    )
    level = np.arange(LEVELS)
    chosen = (level[:, None, None] - level[None, :, None]) % LEVELS == level[None, None, :]
    coefs = jnp.sum(jnp.where(chosen, mixing[:, None, :], 0.0), axis=-1)
    bank = kernels.reshape(kernels.shape[0], VX, PLANE)[:, : VX // 2 + 1]
    twice = np.full((VX // 2 + 1,), 2.0, np.float32)
    twice[0] = twice[VX // 2] = 1.0
    bank = bank * (twice / float(VX * PLANE)).reshape(1, -1, 1)
    bank = jnp.pad(bank, ((0, 0), (0, 0), (0, YZ - PLANE)))
    updated = collide(
        collide_step * own_open, block, bank, coefs, back
    )
    updated = updated.reshape(1, 2, VX, row_width)
    return lax.all_to_all(updated, "vert", split_axis=2, concat_axis=0, tiled=True)


def solution(mesh):
    in_specs = (P("gx", "gy", "vert", None), P(), P(), P(), P())
    out_specs = P("gx", "gy", "vert", None)
    return jax.shard_map(body, mesh=mesh, in_specs=in_specs, out_specs=out_specs, check_vma=False)
```

```python
import math

import ml_dtypes
import numpy as np
import jax
import jax.numpy as jnp
from jax import lax
from jax.experimental import pallas as pl
from jax.experimental.pallas import tpu as pltpu
from jax.sharding import PartitionSpec as P

NX = 64
NY = 16
VX = 24
VY = 24
VZ = 24
LEVELS = 8
PLANE = VY * VZ
HALF = PLANE // 2
SUB = 3
LANES = SUB * HALF
WIDE = 896
YZ = 640
MAIN = 512
DEPTH = 2 * MAIN + 256
HIGH_ORDER = (1, 3, 2)
LOW_ORDER = (0, 2, 1)

courant = 0.45
collide_step = 0.4


def open_share(wall_mask):
    return jnp.where(wall_mask == 1, 0.0, jnp.where(wall_mask == 2, 0.5, 1.0)).astype(jnp.float32)


def cas_matrix(extent):
    counter = np.arange(extent)
    angles = (np.outer(counter, counter) % extent) * (2.0 * np.pi / extent)
    return np.cos(angles) + np.sin(angles)


def speed(index):
    return courant * (2.0 * index - (VX - 1)) / (VX - 1)


def lane_speeds():
    rows = []
    for half in range(2):
        j = np.arange(HALF) // VZ + half * (VY // 2)
        row = np.zeros((WIDE,), np.float32)
        row[:LANES] = np.tile(np.abs(speed(j)), SUB)
        rows.append(np.broadcast_to(row, (LEVELS, WIDE)))
    return np.stack(rows).astype(np.float32)


def minmod(a, b):
    return jnp.maximum(jnp.minimum(a, b), jnp.minimum(jnp.maximum(a, b), 0.0))


def split_kernel(raw, own, to_low, to_high):
    rows_x = raw.shape[0]
    blank = jnp.zeros((LEVELS, WIDE - LANES), jnp.float32)
    for x in range(rows_x):
        for y in range(2):
            wide = [raw[x, i, y].astype(jnp.float32) for i in range(SUB)]
            for half in range(2):
                q = 2 * y + half
                cut = [part[:, half * HALF : (half + 1) * HALF] for part in wide]
                value = jnp.concatenate(cut + [blank], axis=1).astype(jnp.bfloat16)
                own[q, x] = value
                if q in HIGH_ORDER:
                    to_high[HIGH_ORDER.index(q), x] = value
                if q in LOW_ORDER:
                    to_low[LOW_ORDER.index(q), x] = value


def edges_kernel(own, to_down, to_up):
    rows_x = own.shape[1]
    forward = lax.axis_index("vert") >= lax.axis_size("vert") // 2
    for q in range(4):
        for step in range(2):
            row = jnp.where(forward, rows_x - 2 + step, 1 - step)
            to_down[q, step] = own[q, row]
        to_up[q, 0] = own[q, jnp.where(forward, 0, rows_x - 1)]


def edges(own):
    vmem = pl.BlockSpec(memory_space=pltpu.VMEM)
    return pl.pallas_call(
        edges_kernel,
        out_shape=[
            jax.ShapeDtypeStruct((4, count, LEVELS, WIDE), jnp.bfloat16) for count in (2, 1)
        ],
        in_specs=[vmem],
        out_specs=[vmem] * 2,
        compiler_params=pltpu.CompilerParams(vmem_limit_bytes=8 * 1024 * 1024),
        cost_estimate=pl.CostEstimate(flops=100_000, bytes_accessed=400_000, transcendentals=0),
    )(own)


def split(raw):
    rows_x = raw.shape[0]
    vmem = pl.BlockSpec(memory_space=pltpu.VMEM)
    shapes = [(4, rows_x), (3, rows_x), (3, rows_x)]
    return pl.pallas_call(
        split_kernel,
        out_shape=[jax.ShapeDtypeStruct(shape + (LEVELS, WIDE), jnp.bfloat16) for shape in shapes],
        in_specs=[vmem],
        out_specs=[vmem] * 3,
        compiler_params=pltpu.CompilerParams(vmem_limit_bytes=8 * 1024 * 1024),
        cost_estimate=pl.CostEstimate(flops=1_000_000, bytes_accessed=2_000_000, transcendentals=0),
    )(raw)


def open_at(mask, row, column):
    flag = mask[lax.rem(row + NX, NX), lax.rem(column + NY, NY)]
    return jnp.where(flag == 1, 0.0, jnp.where(flag == 2, 0.5, 1.0)).astype(jnp.float32)


def along_x_kernel(flags, mask, own, xup, xdn, speeds_x, part, face_y, face_x):
    rows_x = own.shape[1]
    forward = flags[0] > 0

    def pick(step):
        return jnp.where(forward, step, rows_x - 1 - step)

    for y in range(2):
        cells = [open_at(mask, flags[1] + pick(step), flags[2] + y) for step in range(-1, rows_x + 1)]
        for step in range(rows_x + 1):
            face_x[step, y] = jnp.minimum(cells[step], cells[step + 1])
    for row in range(rows_x):
        cells = [open_at(mask, flags[1] + row, flags[2] + y) for y in range(-1, 3)]
        for face in range(3):
            face_y[row, face] = jnp.minimum(cells[face], cells[face + 1])

    def tile(t, carry):
        lanes = pl.ds(pl.multiple_of(t * 128, 128), 128)
        nu_x = speeds_x[:, lanes]
        half_x = 0.5 * (1.0 - nu_x)
        for q in range(4):
            y = q // 2
            far = xup[q, 0, :, lanes].astype(jnp.float32)
            near = xup[q, 1, :, lanes].astype(jnp.float32)
            now = own[q, pick(0), :, lanes].astype(jnp.float32)
            diff = now - near
            flux = face_x[0, y] * (nu_x * (near + half_x * minmod(near - far, diff)))
            for step in range(rows_x):
                if step + 1 < rows_x:
                    nxt = own[q, pick(step + 1), :, lanes].astype(jnp.float32)
                else:
                    nxt = xdn[q, 0, :, lanes].astype(jnp.float32)
                later = nxt - now
                flux_out = face_x[step + 1, y] * (nu_x * (now + half_x * minmod(diff, later)))
                part[q, pick(step), :, lanes] = now + (flux - flux_out)
                now, diff, flux = nxt, later, flux_out
        return carry

    lax.fori_loop(0, WIDE // 128, tile, 0)


def along_y_kernel(face_y, part, own, low, high_, speeds_y, out):
    rows_x = own.shape[1]

    def tile(t, carry):
        lanes = pl.ds(pl.multiple_of(t * 128, 128), 128)
        for half in range(2):
            nu_y = speeds_y[half, :, lanes]
            half_y = 0.5 * (1.0 - nu_y)
            first, second = (half, 2 + half) if half == 1 else (2 + half, half)
            w0, w1, w2 = (0, 1, 2) if half == 1 else (2, 1, 0)
            for row in range(rows_x):

                def f32(ref, at):
                    return ref[at, row, :, lanes].astype(jnp.float32)

                if half == 1:
                    up2, up1, down = f32(low, 0), f32(low, 1), f32(high_, 2)
                else:
                    up2, up1, down = f32(high_, 1), f32(high_, 0), f32(low, 2)
                a, b = f32(own, first), f32(own, second)
                d0, d1, d2, d3 = up1 - up2, a - up1, b - a, down - b
                g0 = face_y[row, w0] * (nu_y * (up1 + half_y * minmod(d0, d1)))
                g1 = face_y[row, w1] * (nu_y * (a + half_y * minmod(d1, d2)))
                g2 = face_y[row, w2] * (nu_y * (b + half_y * minmod(d2, d3)))
                for at, change in ((first, g0 - g1), (second, g1 - g2)):
                    value = part[at, row, :, lanes] + change
                    out[row, at, :, lanes] = value.astype(jnp.bfloat16)
        return carry

    lax.fori_loop(0, WIDE // 128, tile, 0)


def along_x(flag, mask, own, xup, xdn, speeds_x):
    smem = pl.BlockSpec(memory_space=pltpu.SMEM)
    vmem = pl.BlockSpec(memory_space=pltpu.VMEM)
    return pl.pallas_call(
        along_x_kernel,
        out_shape=[
            jax.ShapeDtypeStruct(own.shape, jnp.float32),
            jax.ShapeDtypeStruct((own.shape[1], 3), jnp.float32),
        ],
        in_specs=[smem] * 2 + [vmem] * 4,
        out_specs=[vmem, smem],
        scratch_shapes=[pltpu.SMEM((own.shape[1] + 1, 2), jnp.float32)],
        compiler_params=pltpu.CompilerParams(vmem_limit_bytes=8 * 1024 * 1024),
        cost_estimate=pl.CostEstimate(flops=5_000_000, bytes_accessed=1_500_000, transcendentals=0),
    )(flag, mask, own, xup, xdn, speeds_x)


def along_y(face_y, part, own, low, high_, speeds_y):
    rows_x = own.shape[1]
    smem = pl.BlockSpec(memory_space=pltpu.SMEM)
    vmem = pl.BlockSpec(memory_space=pltpu.VMEM)
    return pl.pallas_call(
        along_y_kernel,
        out_shape=jax.ShapeDtypeStruct((rows_x, 4, LEVELS, WIDE), jnp.bfloat16),
        in_specs=[smem] + [vmem] * 5,
        out_specs=vmem,
        compiler_params=pltpu.CompilerParams(vmem_limit_bytes=8 * 1024 * 1024),
        cost_estimate=pl.CostEstimate(flops=5_000_000, bytes_accessed=2_500_000, transcendentals=0),
    )(face_y, part, own, low, high_, speeds_y)


def small(matrix, inputs):
    products = {}

    def product(scale, n):
        if scale == 1.0:
            return inputs[n]
        if (scale, n) not in products:
            products[scale, n] = inputs[n] * scale
        return products[scale, n]

    results = []
    for row in matrix:
        total = None
        for n, value in enumerate(row):
            value = round(float(value), 12)
            if value == 0.0:
                continue
            term = product(abs(value), n)
            if total is None:
                total = term if value > 0 else -term
            else:
                total = total + term if value > 0 else total - term
        results.append(total)
    return results


def trig(function, outs, ins, over):
    return [[function(math.pi * k * n / over) for n in ins] for k in outs]


def cosines(v):
    e = [v[n] + v[12 - n] for n in range(6)] + [v[6]]
    o = [v[n] - v[12 - n] for n in range(6)]
    ee = [e[n] + e[6 - n] for n in range(3)] + [e[3]]
    eo = [e[n] - e[6 - n] for n in range(3)]
    out = [None] * 13
    out[0::4] = small(trig(math.cos, range(4), range(4), 3), ee)
    out[2::4] = small(trig(math.cos, (1, 3, 5), range(3), 6), eo)
    out[1::2] = small(trig(math.cos, (1, 3, 5, 7, 9, 11), range(6), 12), o)
    return out


def sines(v):
    v = [None] + v
    f = [v[n] + v[12 - n] for n in range(1, 6)] + [v[6]]
    g = [None] + [v[n] - v[12 - n] for n in range(1, 6)]
    gp = [g[1] + g[5], g[2] + g[4], g[3]]
    gm = [g[1] - g[5], g[2] - g[4]]
    out = [None] * 11
    out[0::2] = small(trig(math.sin, (1, 3, 5, 7, 9, 11), range(1, 7), 12), f)
    out[1::4] = small(trig(math.sin, (1, 3, 5), (1, 2, 3), 6), gp)
    out[3::4] = small(trig(math.sin, (2, 4), (1, 2), 6), gm)
    return out


def modes_of(x):
    even = [x[0]] + [x[n] + x[VX - n] for n in range(1, 12)] + [x[12]]
    odd = [x[n] - x[VX - n] for n in range(1, 12)]
    return cosines(even) + sines(odd)


def points_of(modes):
    p = cosines(modes[:13])
    q = sines(modes[13:])
    out = [None] * VX
    out[0], out[12] = p[0], p[12]
    for n in range(1, 12):
        out[n] = p[n] + q[n - 1]
        out[VX - n] = p[n] - q[n - 1]
    return out


def split_table():
    table = np.kron(cas_matrix(VY), cas_matrix(VZ)).astype(np.float32)
    table = np.pad(table, ((0, 0), (0, YZ - PLANE)))
    top = table.astype(ml_dtypes.bfloat16)
    low = (table - top.astype(np.float32)).astype(ml_dtypes.bfloat16)
    rest = PLANE - MAIN
    back = np.zeros((DEPTH, YZ), ml_dtypes.bfloat16)
    back[0:MAIN] = top[:MAIN]
    back[MAIN : 2 * MAIN] = low[:MAIN]
    back[2 * MAIN : 2 * MAIN + rest] = top[MAIN:PLANE]
    back[2 * MAIN + rest : 2 * MAIN + 2 * rest] = top[MAIN:PLANE]
    back[2 * MAIN + 128 : 2 * MAIN + 128 + rest] = low[MAIN:PLANE]
    return back


def collide_kernel(
    weights, block, bank, coefs, back, out, g, spec, mixed, lhs, left, gain
):
    cells = block.shape[1] // 2
    per_cell = VX * LEVELS
    blank = jnp.zeros((LEVELS, YZ - PLANE), jnp.float32)

    def plane(cell, a):
        source, i = a // SUB, a % SUB
        wide = [block[source, 2 * cell + half].astype(jnp.float32) for half in range(2)]
        cut = [part[:, i * HALF : (i + 1) * HALF] for part in wide]
        return jnp.concatenate(cut + [blank], axis=1)

    for cell in range(cells):
        for m in range(VX // 2):
            pair = jnp.concatenate([plane(cell, 2 * m), plane(cell, 2 * m + 1)], axis=0)
            at_rows = pl.ds(cell * per_cell + 2 * m * LEVELS, 2 * LEVELS)
            g[at_rows, :] = pair.astype(jnp.bfloat16)

    tiles = YZ // 128
    chunks = ((0, 256), (256, 256), (512, 128))

    edge = jnp.concatenate([g[:, MAIN:], g[:, MAIN:]], axis=1)
    for start, width in chunks:
        cols = pl.ds(start, width)
        total = jnp.dot(edge, back[2 * MAIN :, cols], preferred_element_type=jnp.float32)
        for first in (0, MAIN):
            total = total + jnp.dot(
                g[:, :MAIN], back[pl.ds(first, MAIN), cols], preferred_element_type=jnp.float32
            )
        spec[:, cols] = total

    def rows(base, a, count=LEVELS):
        return pl.ds(base + a * LEVELS, count)

    factor = [
        jnp.broadcast_to(coefs[:, shift : shift + 1], (LEVELS, 128)) for shift in range(LEVELS)
    ]

    def ahead(index):
        base, lanes = index // tiles * per_cell, pl.ds(index % tiles * 128, 128)
        modes = modes_of([spec[rows(base, a), lanes] for a in range(VX)])
        for a in range(VX):
            total = factor[0] * modes[a]
            for shift in range(1, LEVELS):
                total = total + factor[shift] * pltpu.roll(modes[a], shift, 0)
            spec[rows(base, a), lanes] = modes[a]
            mixed[rows(base, a), lanes] = total

    for index in range(cells * tiles):
        ahead(index)

    lane = lax.broadcasted_iota(jnp.int32, (2 * LEVELS, 128), 1)

    def prepare(slot, which, source, base, lanes, t, last):
        factors = [bank[which, pl.ds(k, 1), lanes] for k in range(13)]
        points = points_of(
            [source[rows(base, a), lanes] * factors[a if a < 13 else a - 12] for a in range(VX)]
        )
        for m in range(VX // 2):
            pair = jnp.concatenate([points[2 * m], points[2 * m + 1]], axis=0)
            top = pair.astype(jnp.bfloat16)
            rest = pair - top.astype(jnp.float32)
            at_rows = rows(base, 2 * m, 2 * LEVELS)

            def put(start, value):
                lhs[slot, at_rows, pl.ds(start, 128)] = value

            if last:
                both = jnp.where(lane < PLANE - MAIN, pair, pltpu.roll(rest, 64, 1))
                put(2 * MAIN, both.astype(jnp.bfloat16))
                put(2 * MAIN + 128, top)
            else:
                put(t * 128, rest.astype(jnp.bfloat16))
                put(MAIN + t * 128, top)

    def prepare_all(slot, which, source):
        for cell in range(cells):
            for t in range(tiles):
                base = cell * per_cell
                prepare(slot, which, source, base, pl.ds(t * 128, 128), t, t == tiles - 1)

    def product(slot, start, width):
        cols = pl.ds(start, width)
        total = jnp.dot(
            lhs[slot, :, MAIN:], back[MAIN:, cols], preferred_element_type=jnp.float32
        )
        for first in (0, MAIN):
            total = total + jnp.dot(
                lhs[slot, :, pl.ds(first, MAIN)],
                back[:MAIN, cols],
                preferred_element_type=jnp.float32,
            )
        return total

    for direction in range(2):
        prepare_all(2 * direction, direction, spec)
        prepare_all(2 * direction + 1, 2 + direction, mixed)
        for start, width in chunks:
            left[:, pl.ds(start, width)] = product(2 * direction, start, width)
        for start, width in chunks:
            cols = pl.ds(start, width)
            value = left[:, cols] * product(2 * direction + 1, start, width)
            gain[:, cols] = value if direction == 0 else gain[:, cols] + value
    prepare_all(4, 4, mixed)
    for start, width in chunks:
        loss = product(4, start, width)
        for cell in range(cells):
            at_rows = pl.ds(cell * per_cell, per_cell)
            keep = min(width, PLANE - start)
            fields = g[at_rows, pl.ds(start, width)].astype(jnp.float32)
            part = loss[cell * per_cell : (cell + 1) * per_cell]
            value = fields + weights[cell] * (
                gain[at_rows, pl.ds(start, width)] - fields * part
            )
            out[at_rows, pl.ds(start, keep)] = value[:, :keep].astype(jnp.bfloat16)


def resident_kernel(source, out, sem):
    copy = pltpu.make_async_copy(source, out, sem)
    copy.start()
    copy.wait()


def resident(table):
    return pl.pallas_call(
        resident_kernel,
        out_shape=jax.ShapeDtypeStruct(table.shape, table.dtype),
        in_specs=[pl.BlockSpec(memory_space=pl.ANY)],
        out_specs=pl.BlockSpec(memory_space=pltpu.VMEM),
        scratch_shapes=[pltpu.SemaphoreType.DMA],
        compiler_params=pltpu.CompilerParams(vmem_limit_bytes=8 * 1024 * 1024),
        cost_estimate=pl.CostEstimate(flops=0, bytes_accessed=4_600_000, transcendentals=0),
    )(table)


def collide(weights, block, bank, coefs, back):
    count = block.shape[1] // 2 * VX * LEVELS
    smem = pl.BlockSpec(memory_space=pltpu.SMEM)
    vmem = pl.BlockSpec(memory_space=pltpu.VMEM)
    return pl.pallas_call(
        collide_kernel,
        out_shape=jax.ShapeDtypeStruct((count, PLANE), jnp.bfloat16),
        in_specs=[smem] + [vmem] * 4,
        out_specs=vmem,
        scratch_shapes=[
            pltpu.VMEM((count, YZ), jnp.bfloat16),
            pltpu.VMEM((count, YZ), jnp.float32),
            pltpu.VMEM((count, YZ), jnp.float32),
            pltpu.VMEM((5, count, DEPTH), jnp.bfloat16),
            pltpu.VMEM((count, YZ), jnp.float32),
            pltpu.VMEM((count, YZ), jnp.float32),
        ],
        compiler_params=pltpu.CompilerParams(vmem_limit_bytes=16 * 1024 * 1024),
        cost_estimate=pl.CostEstimate(
            flops=8_000_000_000, bytes_accessed=8_000_000, transcendentals=0
        ),
    )(weights, block, bank, coefs, back)


def ring(count, step):
    return [(i, (i + step) % count) for i in range(count)]


def body(distribution, wall_mask, pair_table, trans_weight, kernels):
    rows_x, rows_y, local_vx, row_width = distribution.shape
    count_x = lax.axis_size("gx")
    count_y = lax.axis_size("gy")
    count_v = lax.axis_size("vert")
    at_v = lax.axis_index("vert")
    forward = at_v >= count_v // 2

    anchor_x = lax.axis_index("gx") * rows_x
    anchor_y = lax.axis_index("gy") * rows_y
    flag = jnp.stack([forward.astype(jnp.int32), anchor_x, anchor_y])
    raw = distribution.transpose(0, 2, 1, 3).reshape(rows_x, SUB, 2, LEVELS, PLANE)
    own, to_low, to_high = split(raw)
    low = lax.ppermute(to_high, "gy", ring(count_y, 1))
    high_ = lax.ppermute(to_low, "gy", ring(count_y, -1))

    index_x = at_v * local_vx + jnp.arange(WIDE, dtype=jnp.int32) // HALF
    speeds_x = jnp.abs(speed(index_x.astype(jnp.float32)))
    upstream, downstream = edges(own)
    send_up, send_down = [], []
    for i in range(count_x):
        for v in range(count_v):
            step = 1 if v >= count_v // 2 else -1
            send_up.append((i * count_v + v, (i + step) % count_x * count_v + v))
            send_down.append((i * count_v + v, (i - step) % count_x * count_v + v))
    xup = lax.ppermute(upstream, ("gx", "vert"), send_up)
    xdn = lax.ppermute(downstream, ("gx", "vert"), send_down)

    openness = open_share(wall_mask)
    own_open = lax.dynamic_slice(openness, (anchor_x + at_v, anchor_y), (1, rows_y))[0]

    speeds_x = jnp.broadcast_to(speeds_x[None], (LEVELS, WIDE))
    speeds_y = jnp.asarray(lane_speeds())
    part, face_y = along_x(flag, wall_mask, own, xup, xdn, speeds_x)
    transported = along_y(face_y, part, own, low, high_, speeds_y)

    back = jnp.asarray(split_table())
    block = lax.all_to_all(transported, "vert", split_axis=0, concat_axis=0, tiled=True)
    entries = jnp.arange(trans_weight.shape[0], dtype=jnp.int32)
    mixing = jnp.sum(
        jnp.where(
            pair_table[:, :, None] == entries[None, None, :], trans_weight[None, None, :], 0.0
        ),
        axis=-1,
    )
    level = np.arange(LEVELS)
    chosen = (level[:, None, None] - level[None, :, None]) % LEVELS == level[None, None, :]
    coefs = jnp.sum(jnp.where(chosen, mixing[:, None, :], 0.0), axis=-1)
    bank = kernels.reshape(kernels.shape[0], VX, PLANE)[:, : VX // 2 + 1]
    twice = np.full((VX // 2 + 1,), 2.0, np.float32)
    twice[0] = twice[VX // 2] = 1.0
    bank = bank * (twice / float(VX * PLANE)).reshape(1, -1, 1)
    bank = jnp.pad(bank, ((0, 0), (0, 0), (0, YZ - PLANE)))
    updated = collide(
        collide_step * own_open, block, bank, coefs, back
    )
    updated = updated.reshape(1, 2, VX, row_width)
    return lax.all_to_all(updated, "vert", split_axis=2, concat_axis=0, tiled=True)


def solution(mesh):
    in_specs = (P("gx", "gy", "vert", None), P(), P(), P(), P())
    out_specs = P("gx", "gy", "vert", None)
    return jax.shard_map(body, mesh=mesh, in_specs=in_specs, out_specs=out_specs, check_vma=False)
```

```python
import math

import ml_dtypes
import numpy as np
import jax
import jax.numpy as jnp
from jax import lax
from jax.experimental import pallas as pl
from jax.experimental.pallas import tpu as pltpu
from jax.sharding import PartitionSpec as P

NX = 64
NY = 16
VX = 24
VY = 24
VZ = 24
LEVELS = 8
PLANE = VY * VZ
HALF = PLANE // 2
SUB = 3
LANES = SUB * HALF
WIDE = 896
YZ = 640
MAIN = 512
DEPTH = 2 * MAIN + 256
HIGH_ORDER = (1, 3, 2)
LOW_ORDER = (0, 2, 1)

courant = 0.45
collide_step = 0.4


def open_share(wall_mask):
    return jnp.where(wall_mask == 1, 0.0, jnp.where(wall_mask == 2, 0.5, 1.0)).astype(jnp.float32)


def cas_matrix(extent):
    counter = np.arange(extent)
    angles = (np.outer(counter, counter) % extent) * (2.0 * np.pi / extent)
    return np.cos(angles) + np.sin(angles)


def speed(index):
    return courant * (2.0 * index - (VX - 1)) / (VX - 1)


def lane_speeds():
    rows = []
    for half in range(2):
        j = np.arange(HALF) // VZ + half * (VY // 2)
        row = np.zeros((WIDE,), np.float32)
        row[:LANES] = np.tile(np.abs(speed(j)), SUB)
        rows.append(np.broadcast_to(row, (LEVELS, WIDE)))
    return np.stack(rows).astype(np.float32)


def minmod(a, b):
    return jnp.maximum(jnp.minimum(a, b), jnp.minimum(jnp.maximum(a, b), 0.0))


def split_kernel(raw, own, to_low, to_high):
    rows_x = raw.shape[0]
    blank = jnp.zeros((LEVELS, WIDE - LANES), jnp.float32)
    for x in range(rows_x):
        for y in range(2):
            wide = [raw[x, i, y].astype(jnp.float32) for i in range(SUB)]
            for half in range(2):
                q = 2 * y + half
                cut = [part[:, half * HALF : (half + 1) * HALF] for part in wide]
                value = jnp.concatenate(cut + [blank], axis=1).astype(jnp.bfloat16)
                own[q, x] = value
                if q in HIGH_ORDER:
                    to_high[HIGH_ORDER.index(q), x] = value
                if q in LOW_ORDER:
                    to_low[LOW_ORDER.index(q), x] = value


def edges_kernel(own, to_down, to_up):
    rows_x = own.shape[1]
    forward = lax.axis_index("vert") >= lax.axis_size("vert") // 2
    for q in range(4):
        for step in range(2):
            row = jnp.where(forward, rows_x - 2 + step, 1 - step)
            to_down[q, step] = own[q, row]
        to_up[q, 0] = own[q, jnp.where(forward, 0, rows_x - 1)]


def edges(own):
    vmem = pl.BlockSpec(memory_space=pltpu.VMEM)
    return pl.pallas_call(
        edges_kernel,
        out_shape=[
            jax.ShapeDtypeStruct((4, count, LEVELS, WIDE), jnp.bfloat16) for count in (2, 1)
        ],
        in_specs=[vmem],
        out_specs=[vmem] * 2,
        compiler_params=pltpu.CompilerParams(vmem_limit_bytes=8 * 1024 * 1024),
        cost_estimate=pl.CostEstimate(flops=100_000, bytes_accessed=400_000, transcendentals=0),
    )(own)


def split(raw):
    rows_x = raw.shape[0]
    vmem = pl.BlockSpec(memory_space=pltpu.VMEM)
    shapes = [(4, rows_x), (3, rows_x), (3, rows_x)]
    return pl.pallas_call(
        split_kernel,
        out_shape=[jax.ShapeDtypeStruct(shape + (LEVELS, WIDE), jnp.bfloat16) for shape in shapes],
        in_specs=[vmem],
        out_specs=[vmem] * 3,
        compiler_params=pltpu.CompilerParams(vmem_limit_bytes=8 * 1024 * 1024),
        cost_estimate=pl.CostEstimate(flops=1_000_000, bytes_accessed=2_000_000, transcendentals=0),
    )(raw)


def open_at(mask, row, column):
    flag = mask[lax.rem(row + NX, NX), lax.rem(column + NY, NY)]
    return jnp.where(flag == 1, 0.0, jnp.where(flag == 2, 0.5, 1.0)).astype(jnp.float32)


def faces_kernel(flags, mask, face_x, face_y):
    rows_x = face_y.shape[0]
    forward = flags[0] > 0

    def pick(step):
        return jnp.where(forward, step, rows_x - 1 - step)

    for y in range(2):
        cells = [open_at(mask, flags[1] + pick(step), flags[2] + y) for step in range(-1, rows_x + 1)]
        for step in range(rows_x + 1):
            face_x[step, y] = jnp.minimum(cells[step], cells[step + 1])
    for row in range(rows_x):
        cells = [open_at(mask, flags[1] + row, flags[2] + y) for y in range(-1, 3)]
        for face in range(3):
            face_y[row, face] = jnp.minimum(cells[face], cells[face + 1])


def faces(flag, mask, rows_x):
    smem = pl.BlockSpec(memory_space=pltpu.SMEM)
    return pl.pallas_call(
        faces_kernel,
        out_shape=[
            jax.ShapeDtypeStruct((rows_x + 1, 2), jnp.float32),
            jax.ShapeDtypeStruct((rows_x, 3), jnp.float32),
        ],
        in_specs=[smem] * 2,
        out_specs=[smem] * 2,
        compiler_params=pltpu.CompilerParams(vmem_limit_bytes=8 * 1024 * 1024),
        cost_estimate=pl.CostEstimate(flops=1_000, bytes_accessed=10_000, transcendentals=0),
    )(flag, mask)


def along_x_kernel(face_x, own, xup, xdn, speeds_x, part):
    rows_x = own.shape[1]
    forward = lax.axis_index("vert") >= lax.axis_size("vert") // 2

    def pick(step):
        return jnp.where(forward, step, rows_x - 1 - step)

    def tile(t, carry):
        lanes = pl.ds(pl.multiple_of(t * 128, 128), 128)
        nu_x = speeds_x[:, lanes]
        half_x = 0.5 * (1.0 - nu_x)
        for q in range(4):
            y = q // 2
            far = xup[q, 0, :, lanes].astype(jnp.float32)
            near = xup[q, 1, :, lanes].astype(jnp.float32)
            now = own[q, pick(0), :, lanes].astype(jnp.float32)
            diff = now - near
            flux = face_x[0, y] * (nu_x * (near + half_x * minmod(near - far, diff)))
            for step in range(rows_x):
                if step + 1 < rows_x:
                    nxt = own[q, pick(step + 1), :, lanes].astype(jnp.float32)
                else:
                    nxt = xdn[q, 0, :, lanes].astype(jnp.float32)
                later = nxt - now
                flux_out = face_x[step + 1, y] * (nu_x * (now + half_x * minmod(diff, later)))
                part[q, pick(step), :, lanes] = now + (flux - flux_out)
                now, diff, flux = nxt, later, flux_out
        return carry

    lax.fori_loop(0, WIDE // 128, tile, 0)


def along_y_kernel(face_y, part, own, low, high_, speeds_y, out):
    rows_x = own.shape[1]

    def tile(t, carry):
        lanes = pl.ds(pl.multiple_of(t * 128, 128), 128)
        for half in range(2):
            nu_y = speeds_y[half, :, lanes]
            half_y = 0.5 * (1.0 - nu_y)
            first, second = (half, 2 + half) if half == 1 else (2 + half, half)
            w0, w1, w2 = (0, 1, 2) if half == 1 else (2, 1, 0)
            for row in range(rows_x):

                def f32(ref, at):
                    return ref[at, row, :, lanes].astype(jnp.float32)

                if half == 1:
                    up2, up1, down = f32(low, 0), f32(low, 1), f32(high_, 2)
                else:
                    up2, up1, down = f32(high_, 1), f32(high_, 0), f32(low, 2)
                a, b = f32(own, first), f32(own, second)
                d0, d1, d2, d3 = up1 - up2, a - up1, b - a, down - b
                g0 = face_y[row, w0] * (nu_y * (up1 + half_y * minmod(d0, d1)))
                g1 = face_y[row, w1] * (nu_y * (a + half_y * minmod(d1, d2)))
                g2 = face_y[row, w2] * (nu_y * (b + half_y * minmod(d2, d3)))
                for at, change in ((first, g0 - g1), (second, g1 - g2)):
                    value = part[at, row, :, lanes] + change
                    out[row, at, :, lanes] = value.astype(jnp.bfloat16)
        return carry

    lax.fori_loop(0, WIDE // 128, tile, 0)


def along_x(face_x, own, xup, xdn, speeds_x):
    smem = pl.BlockSpec(memory_space=pltpu.SMEM)
    vmem = pl.BlockSpec(memory_space=pltpu.VMEM)
    return pl.pallas_call(
        along_x_kernel,
        out_shape=jax.ShapeDtypeStruct(own.shape, jnp.float32),
        in_specs=[smem] + [vmem] * 4,
        out_specs=vmem,
        compiler_params=pltpu.CompilerParams(vmem_limit_bytes=8 * 1024 * 1024),
        cost_estimate=pl.CostEstimate(flops=5_000_000, bytes_accessed=1_500_000, transcendentals=0),
    )(face_x, own, xup, xdn, speeds_x)


def along_y(face_y, part, own, low, high_, speeds_y):
    rows_x = own.shape[1]
    smem = pl.BlockSpec(memory_space=pltpu.SMEM)
    vmem = pl.BlockSpec(memory_space=pltpu.VMEM)
    return pl.pallas_call(
        along_y_kernel,
        out_shape=jax.ShapeDtypeStruct((rows_x, 4, LEVELS, WIDE), jnp.bfloat16),
        in_specs=[smem] + [vmem] * 5,
        out_specs=vmem,
        compiler_params=pltpu.CompilerParams(vmem_limit_bytes=8 * 1024 * 1024),
        cost_estimate=pl.CostEstimate(flops=5_000_000, bytes_accessed=2_500_000, transcendentals=0),
    )(face_y, part, own, low, high_, speeds_y)


def small(matrix, inputs):
    products = {}

    def product(scale, n):
        if scale == 1.0:
            return inputs[n]
        if (scale, n) not in products:
            products[scale, n] = inputs[n] * scale
        return products[scale, n]

    results = []
    for row in matrix:
        total = None
        for n, value in enumerate(row):
            value = round(float(value), 12)
            if value == 0.0:
                continue
            term = product(abs(value), n)
            if total is None:
                total = term if value > 0 else -term
            else:
                total = total + term if value > 0 else total - term
        results.append(total)
    return results


def trig(function, outs, ins, over):
    return [[function(math.pi * k * n / over) for n in ins] for k in outs]


def cosines(v):
    e = [v[n] + v[12 - n] for n in range(6)] + [v[6]]
    o = [v[n] - v[12 - n] for n in range(6)]
    ee = [e[n] + e[6 - n] for n in range(3)] + [e[3]]
    eo = [e[n] - e[6 - n] for n in range(3)]
    out = [None] * 13
    out[0::4] = small(trig(math.cos, range(4), range(4), 3), ee)
    out[2::4] = small(trig(math.cos, (1, 3, 5), range(3), 6), eo)
    out[1::2] = small(trig(math.cos, (1, 3, 5, 7, 9, 11), range(6), 12), o)
    return out


def sines(v):
    v = [None] + v
    f = [v[n] + v[12 - n] for n in range(1, 6)] + [v[6]]
    g = [None] + [v[n] - v[12 - n] for n in range(1, 6)]
    gp = [g[1] + g[5], g[2] + g[4], g[3]]
    gm = [g[1] - g[5], g[2] - g[4]]
    out = [None] * 11
    out[0::2] = small(trig(math.sin, (1, 3, 5, 7, 9, 11), range(1, 7), 12), f)
    out[1::4] = small(trig(math.sin, (1, 3, 5), (1, 2, 3), 6), gp)
    out[3::4] = small(trig(math.sin, (2, 4), (1, 2), 6), gm)
    return out


def modes_of(x):
    even = [x[0]] + [x[n] + x[VX - n] for n in range(1, 12)] + [x[12]]
    odd = [x[n] - x[VX - n] for n in range(1, 12)]
    return cosines(even) + sines(odd)


def points_of(modes):
    p = cosines(modes[:13])
    q = sines(modes[13:])
    out = [None] * VX
    out[0], out[12] = p[0], p[12]
    for n in range(1, 12):
        out[n] = p[n] + q[n - 1]
        out[VX - n] = p[n] - q[n - 1]
    return out


def split_table():
    table = np.kron(cas_matrix(VY), cas_matrix(VZ)).astype(np.float32)
    table = np.pad(table, ((0, 0), (0, YZ - PLANE)))
    top = table.astype(ml_dtypes.bfloat16)
    low = (table - top.astype(np.float32)).astype(ml_dtypes.bfloat16)
    rest = PLANE - MAIN
    back = np.zeros((DEPTH, YZ), ml_dtypes.bfloat16)
    back[0:MAIN] = top[:MAIN]
    back[MAIN : 2 * MAIN] = low[:MAIN]
    back[2 * MAIN : 2 * MAIN + rest] = top[MAIN:PLANE]
    back[2 * MAIN + rest : 2 * MAIN + 2 * rest] = top[MAIN:PLANE]
    back[2 * MAIN + 128 : 2 * MAIN + 128 + rest] = low[MAIN:PLANE]
    return back


def collide_kernel(
    weights, block, bank, coefs, back, out, g, spec, mixed, lhs, left, gain
):
    cells = block.shape[1] // 2
    per_cell = VX * LEVELS
    blank = jnp.zeros((LEVELS, YZ - PLANE), jnp.float32)

    def plane(cell, a):
        source, i = a // SUB, a % SUB
        wide = [block[source, 2 * cell + half].astype(jnp.float32) for half in range(2)]
        cut = [part[:, i * HALF : (i + 1) * HALF] for part in wide]
        return jnp.concatenate(cut + [blank], axis=1)

    for cell in range(cells):
        for m in range(VX // 2):
            pair = jnp.concatenate([plane(cell, 2 * m), plane(cell, 2 * m + 1)], axis=0)
            at_rows = pl.ds(cell * per_cell + 2 * m * LEVELS, 2 * LEVELS)
            g[at_rows, :] = pair.astype(jnp.bfloat16)

    tiles = YZ // 128
    chunks = ((0, 256), (256, 256), (512, 128))

    edge = jnp.concatenate([g[:, MAIN:], g[:, MAIN:]], axis=1)
    for start, width in chunks:
        cols = pl.ds(start, width)
        total = jnp.dot(edge, back[2 * MAIN :, cols], preferred_element_type=jnp.float32)
        for first in (0, MAIN):
            total = total + jnp.dot(
                g[:, :MAIN], back[pl.ds(first, MAIN), cols], preferred_element_type=jnp.float32
            )
        spec[:, cols] = total

    def rows(base, a, count=LEVELS):
        return pl.ds(base + a * LEVELS, count)

    factor = [
        jnp.broadcast_to(coefs[:, shift : shift + 1], (LEVELS, 128)) for shift in range(LEVELS)
    ]

    def ahead(index):
        base, lanes = index // tiles * per_cell, pl.ds(index % tiles * 128, 128)
        modes = modes_of([spec[rows(base, a), lanes] for a in range(VX)])
        for a in range(VX):
            total = factor[0] * modes[a]
            for shift in range(1, LEVELS):
                total = total + factor[shift] * pltpu.roll(modes[a], shift, 0)
            spec[rows(base, a), lanes] = modes[a]
            mixed[rows(base, a), lanes] = total

    for index in range(cells * tiles):
        ahead(index)

    lane = lax.broadcasted_iota(jnp.int32, (2 * LEVELS, 128), 1)

    def prepare(slot, which, source, base, lanes, t, last):
        factors = [bank[which, pl.ds(k, 1), lanes] for k in range(13)]
        points = points_of(
            [source[rows(base, a), lanes] * factors[a if a < 13 else a - 12] for a in range(VX)]
        )
        for m in range(VX // 2):
            pair = jnp.concatenate([points[2 * m], points[2 * m + 1]], axis=0)
            top = pair.astype(jnp.bfloat16)
            rest = pair - top.astype(jnp.float32)
            at_rows = rows(base, 2 * m, 2 * LEVELS)

            def put(start, value):
                lhs[slot, at_rows, pl.ds(start, 128)] = value

            if last:
                both = jnp.where(lane < PLANE - MAIN, pair, pltpu.roll(rest, 64, 1))
                put(2 * MAIN, both.astype(jnp.bfloat16))
                put(2 * MAIN + 128, top)
            else:
                put(t * 128, rest.astype(jnp.bfloat16))
                put(MAIN + t * 128, top)

    def prepare_all(slot, which, source):
        for cell in range(cells):
            for t in range(tiles):
                base = cell * per_cell
                prepare(slot, which, source, base, pl.ds(t * 128, 128), t, t == tiles - 1)

    def product(slot, start, width):
        cols = pl.ds(start, width)
        total = jnp.dot(
            lhs[slot, :, MAIN:], back[MAIN:, cols], preferred_element_type=jnp.float32
        )
        for first in (0, MAIN):
            total = total + jnp.dot(
                lhs[slot, :, pl.ds(first, MAIN)],
                back[:MAIN, cols],
                preferred_element_type=jnp.float32,
            )
        return total

    for direction in range(2):
        prepare_all(2 * direction, direction, spec)
        prepare_all(2 * direction + 1, 2 + direction, mixed)
        for start, width in chunks:
            left[:, pl.ds(start, width)] = product(2 * direction, start, width)
        for start, width in chunks:
            cols = pl.ds(start, width)
            value = left[:, cols] * product(2 * direction + 1, start, width)
            gain[:, cols] = value if direction == 0 else gain[:, cols] + value
    prepare_all(4, 4, mixed)
    for start, width in chunks:
        loss = product(4, start, width)
        for cell in range(cells):
            at_rows = pl.ds(cell * per_cell, per_cell)
            keep = min(width, PLANE - start)
            fields = g[at_rows, pl.ds(start, width)].astype(jnp.float32)
            part = loss[cell * per_cell : (cell + 1) * per_cell]
            value = fields + weights[cell] * (
                gain[at_rows, pl.ds(start, width)] - fields * part
            )
            out[at_rows, pl.ds(start, keep)] = value[:, :keep].astype(jnp.bfloat16)


def resident_kernel(source, out, sem):
    copy = pltpu.make_async_copy(source, out, sem)
    copy.start()
    copy.wait()


def resident(table):
    return pl.pallas_call(
        resident_kernel,
        out_shape=jax.ShapeDtypeStruct(table.shape, table.dtype),
        in_specs=[pl.BlockSpec(memory_space=pl.ANY)],
        out_specs=pl.BlockSpec(memory_space=pltpu.VMEM),
        scratch_shapes=[pltpu.SemaphoreType.DMA],
        compiler_params=pltpu.CompilerParams(vmem_limit_bytes=8 * 1024 * 1024),
        cost_estimate=pl.CostEstimate(flops=0, bytes_accessed=4_600_000, transcendentals=0),
    )(table)


def collide(weights, block, bank, coefs, back):
    count = block.shape[1] // 2 * VX * LEVELS
    smem = pl.BlockSpec(memory_space=pltpu.SMEM)
    vmem = pl.BlockSpec(memory_space=pltpu.VMEM)
    return pl.pallas_call(
        collide_kernel,
        out_shape=jax.ShapeDtypeStruct((count, PLANE), jnp.bfloat16),
        in_specs=[smem] + [vmem] * 4,
        out_specs=vmem,
        scratch_shapes=[
            pltpu.VMEM((count, YZ), jnp.bfloat16),
            pltpu.VMEM((count, YZ), jnp.float32),
            pltpu.VMEM((count, YZ), jnp.float32),
            pltpu.VMEM((5, count, DEPTH), jnp.bfloat16),
            pltpu.VMEM((count, YZ), jnp.float32),
            pltpu.VMEM((count, YZ), jnp.float32),
        ],
        compiler_params=pltpu.CompilerParams(vmem_limit_bytes=16 * 1024 * 1024),
        cost_estimate=pl.CostEstimate(
            flops=8_000_000_000, bytes_accessed=8_000_000, transcendentals=0
        ),
    )(weights, block, bank, coefs, back)


def ring(count, step):
    return [(i, (i + step) % count) for i in range(count)]


def body(distribution, wall_mask, pair_table, trans_weight, kernels):
    rows_x, rows_y, local_vx, row_width = distribution.shape
    count_x = lax.axis_size("gx")
    count_y = lax.axis_size("gy")
    count_v = lax.axis_size("vert")
    at_v = lax.axis_index("vert")
    forward = at_v >= count_v // 2

    anchor_x = lax.axis_index("gx") * rows_x
    anchor_y = lax.axis_index("gy") * rows_y
    flag = jnp.stack([forward.astype(jnp.int32), anchor_x, anchor_y])
    raw = distribution.transpose(0, 2, 1, 3).reshape(rows_x, SUB, 2, LEVELS, PLANE)
    own, to_low, to_high = split(raw)
    low = lax.ppermute(to_high, "gy", ring(count_y, 1))
    high_ = lax.ppermute(to_low, "gy", ring(count_y, -1))

    index_x = at_v * local_vx + jnp.arange(WIDE, dtype=jnp.int32) // HALF
    speeds_x = jnp.abs(speed(index_x.astype(jnp.float32)))
    upstream, downstream = edges(own)
    send_up, send_down = [], []
    for i in range(count_x):
        for v in range(count_v):
            step = 1 if v >= count_v // 2 else -1
            send_up.append((i * count_v + v, (i + step) % count_x * count_v + v))
            send_down.append((i * count_v + v, (i - step) % count_x * count_v + v))
    xup = lax.ppermute(upstream, ("gx", "vert"), send_up)
    xdn = lax.ppermute(downstream, ("gx", "vert"), send_down)

    openness = open_share(wall_mask)
    own_open = lax.dynamic_slice(openness, (anchor_x + at_v, anchor_y), (1, rows_y))[0]

    speeds_x = jnp.broadcast_to(speeds_x[None], (LEVELS, WIDE))
    speeds_y = jnp.asarray(lane_speeds())
    face_x, face_y = faces(flag, wall_mask, rows_x)
    part = along_x(face_x, own, xup, xdn, speeds_x)
    transported = along_y(face_y, part, own, low, high_, speeds_y)

    back = jnp.asarray(split_table())
    block = lax.all_to_all(transported, "vert", split_axis=0, concat_axis=0, tiled=True)
    entries = jnp.arange(trans_weight.shape[0], dtype=jnp.int32)
    mixing = jnp.sum(
        jnp.where(
            pair_table[:, :, None] == entries[None, None, :], trans_weight[None, None, :], 0.0
        ),
        axis=-1,
    )
    level = np.arange(LEVELS)
    chosen = (level[:, None, None] - level[None, :, None]) % LEVELS == level[None, None, :]
    coefs = jnp.sum(jnp.where(chosen, mixing[:, None, :], 0.0), axis=-1)
    bank = kernels.reshape(kernels.shape[0], VX, PLANE)[:, : VX // 2 + 1]
    twice = np.full((VX // 2 + 1,), 2.0, np.float32)
    twice[0] = twice[VX // 2] = 1.0
    bank = bank * (twice / float(VX * PLANE)).reshape(1, -1, 1)
    bank = jnp.pad(bank, ((0, 0), (0, 0), (0, YZ - PLANE)))
    updated = collide(
        collide_step * own_open, block, bank, coefs, back
    )
    updated = updated.reshape(1, 2, VX, row_width)
    return lax.all_to_all(updated, "vert", split_axis=2, concat_axis=0, tiled=True)


def solution(mesh):
    in_specs = (P("gx", "gy", "vert", None), P(), P(), P(), P())
    out_specs = P("gx", "gy", "vert", None)
    return jax.shard_map(body, mesh=mesh, in_specs=in_specs, out_specs=out_specs, check_vma=False)
```

```python
import math

import ml_dtypes
import numpy as np
import jax
import jax.numpy as jnp
from jax import lax
from jax.experimental import pallas as pl
from jax.experimental.pallas import tpu as pltpu
from jax.sharding import PartitionSpec as P

NX = 64
NY = 16
VX = 24
VY = 24
VZ = 24
LEVELS = 8
PLANE = VY * VZ
HALF = PLANE // 2
SUB = 3
LANES = SUB * HALF
WIDE = 896
YZ = 640
MAIN = 512
DEPTH = 2 * MAIN + 256
HIGH_ORDER = (1, 3, 2)
LOW_ORDER = (0, 2, 1)

courant = 0.45
collide_step = 0.4


def open_share(wall_mask):
    return jnp.where(wall_mask == 1, 0.0, jnp.where(wall_mask == 2, 0.5, 1.0)).astype(jnp.float32)


def cas_matrix(extent):
    counter = np.arange(extent)
    angles = (np.outer(counter, counter) % extent) * (2.0 * np.pi / extent)
    return np.cos(angles) + np.sin(angles)


def speed(index):
    return courant * (2.0 * index - (VX - 1)) / (VX - 1)


def lane_speeds():
    rows = []
    for half in range(2):
        j = np.arange(HALF) // VZ + half * (VY // 2)
        row = np.zeros((WIDE,), np.float32)
        row[:LANES] = np.tile(np.abs(speed(j)), SUB)
        rows.append(np.broadcast_to(row, (LEVELS, WIDE)))
    return np.stack(rows).astype(np.float32)


def minmod(a, b):
    return jnp.maximum(jnp.minimum(a, b), jnp.minimum(jnp.maximum(a, b), 0.0))


def split_kernel(raw, own, to_low, to_high):
    rows_x = raw.shape[0]
    blank = jnp.zeros((LEVELS, WIDE - LANES), jnp.float32)
    for x in range(rows_x):
        for y in range(2):
            wide = [raw[x, i, y].astype(jnp.float32) for i in range(SUB)]
            for half in range(2):
                q = 2 * y + half
                cut = [part[:, half * HALF : (half + 1) * HALF] for part in wide]
                value = jnp.concatenate(cut + [blank], axis=1).astype(jnp.bfloat16)
                own[q, x] = value
                if q in HIGH_ORDER:
                    to_high[HIGH_ORDER.index(q), x] = value
                if q in LOW_ORDER:
                    to_low[LOW_ORDER.index(q), x] = value


def edges_kernel(own, to_down, to_up):
    rows_x = own.shape[1]
    forward = lax.axis_index("vert") >= lax.axis_size("vert") // 2
    for q in range(4):
        for step in range(2):
            row = jnp.where(forward, rows_x - 2 + step, 1 - step)
            to_down[q, step] = own[q, row]
        to_up[q, 0] = own[q, jnp.where(forward, 0, rows_x - 1)]


def edges(own):
    vmem = pl.BlockSpec(memory_space=pltpu.VMEM)
    return pl.pallas_call(
        edges_kernel,
        out_shape=[
            jax.ShapeDtypeStruct((4, count, LEVELS, WIDE), jnp.bfloat16) for count in (2, 1)
        ],
        in_specs=[vmem],
        out_specs=[vmem] * 2,
        compiler_params=pltpu.CompilerParams(vmem_limit_bytes=8 * 1024 * 1024),
        cost_estimate=pl.CostEstimate(flops=100_000, bytes_accessed=400_000, transcendentals=0),
    )(own)


def split(raw):
    rows_x = raw.shape[0]
    vmem = pl.BlockSpec(memory_space=pltpu.VMEM)
    shapes = [(4, rows_x), (3, rows_x), (3, rows_x)]
    return pl.pallas_call(
        split_kernel,
        out_shape=[jax.ShapeDtypeStruct(shape + (LEVELS, WIDE), jnp.bfloat16) for shape in shapes],
        in_specs=[vmem],
        out_specs=[vmem] * 3,
        compiler_params=pltpu.CompilerParams(vmem_limit_bytes=8 * 1024 * 1024),
        cost_estimate=pl.CostEstimate(flops=1_000_000, bytes_accessed=2_000_000, transcendentals=0),
    )(raw)


def open_at(mask, row, column):
    flag = mask[lax.rem(row + NX, NX), lax.rem(column + NY, NY)]
    return jnp.where(flag == 1, 0.0, jnp.where(flag == 2, 0.5, 1.0)).astype(jnp.float32)


def faces_kernel(flags, mask, face_x, face_y):
    rows_x = face_y.shape[0]
    forward = flags[0] > 0

    def pick(step):
        return jnp.where(forward, step, rows_x - 1 - step)

    for y in range(2):
        cells = [open_at(mask, flags[1] + pick(step), flags[2] + y) for step in range(-1, rows_x + 1)]
        for step in range(rows_x + 1):
            face_x[step, y] = jnp.minimum(cells[step], cells[step + 1])
    for row in range(rows_x):
        cells = [open_at(mask, flags[1] + row, flags[2] + y) for y in range(-1, 3)]
        for face in range(3):
            face_y[row, face] = jnp.minimum(cells[face], cells[face + 1])


def faces(flag, mask, rows_x):
    smem = pl.BlockSpec(memory_space=pltpu.SMEM)
    return pl.pallas_call(
        faces_kernel,
        out_shape=[
            jax.ShapeDtypeStruct((rows_x + 1, 2), jnp.float32),
            jax.ShapeDtypeStruct((rows_x, 3), jnp.float32),
        ],
        in_specs=[smem] * 2,
        out_specs=[smem] * 2,
        compiler_params=pltpu.CompilerParams(vmem_limit_bytes=8 * 1024 * 1024),
        cost_estimate=pl.CostEstimate(flops=1_000, bytes_accessed=10_000, transcendentals=0),
    )(flag, mask)


def along_x_kernel(face_x, own, xup, xdn, speeds_x, part):
    rows_x = own.shape[1]
    forward = lax.axis_index("vert") >= lax.axis_size("vert") // 2

    def pick(step):
        return jnp.where(forward, step, rows_x - 1 - step)

    def tile(t, carry):
        lanes = pl.ds(pl.multiple_of(t * 128, 128), 128)
        nu_x = speeds_x[:, lanes]
        half_x = 0.5 * (1.0 - nu_x)
        for q in range(4):
            y = q // 2
            far = xup[q, 0, :, lanes].astype(jnp.float32)
            near = xup[q, 1, :, lanes].astype(jnp.float32)
            now = own[q, pick(0), :, lanes].astype(jnp.float32)
            diff = now - near
            flux = face_x[0, y] * (nu_x * (near + half_x * minmod(near - far, diff)))
            for step in range(rows_x):
                if step + 1 < rows_x:
                    nxt = own[q, pick(step + 1), :, lanes].astype(jnp.float32)
                else:
                    nxt = xdn[q, 0, :, lanes].astype(jnp.float32)
                later = nxt - now
                flux_out = face_x[step + 1, y] * (nu_x * (now + half_x * minmod(diff, later)))
                part[q, pick(step), :, lanes] = now + (flux - flux_out)
                now, diff, flux = nxt, later, flux_out
        return carry

    lax.fori_loop(0, WIDE // 128, tile, 0)


def along_y_kernel(face_y, part, own, low, high_, speeds_y, out):
    rows_x = own.shape[1]

    def tile(t, carry):
        lanes = pl.ds(pl.multiple_of(t * 128, 128), 128)
        for half in range(2):
            nu_y = speeds_y[half, :, lanes]
            half_y = 0.5 * (1.0 - nu_y)
            first, second = (half, 2 + half) if half == 1 else (2 + half, half)
            w0, w1, w2 = (0, 1, 2) if half == 1 else (2, 1, 0)
            for row in range(rows_x):

                def f32(ref, at):
                    return ref[at, row, :, lanes].astype(jnp.float32)

                if half == 1:
                    up2, up1, down = f32(low, 0), f32(low, 1), f32(high_, 2)
                else:
                    up2, up1, down = f32(high_, 1), f32(high_, 0), f32(low, 2)
                a, b = f32(own, first), f32(own, second)
                d0, d1, d2, d3 = up1 - up2, a - up1, b - a, down - b
                g0 = face_y[row, w0] * (nu_y * (up1 + half_y * minmod(d0, d1)))
                g1 = face_y[row, w1] * (nu_y * (a + half_y * minmod(d1, d2)))
                g2 = face_y[row, w2] * (nu_y * (b + half_y * minmod(d2, d3)))
                for at, change in ((first, g0 - g1), (second, g1 - g2)):
                    value = part[at, row, :, lanes] + change
                    out[row, at, :, lanes] = value.astype(jnp.bfloat16)
        return carry

    lax.fori_loop(0, WIDE // 128, tile, 0)


def along_x(face_x, own, xup, xdn, speeds_x):
    smem = pl.BlockSpec(memory_space=pltpu.SMEM)
    vmem = pl.BlockSpec(memory_space=pltpu.VMEM)
    return pl.pallas_call(
        along_x_kernel,
        out_shape=jax.ShapeDtypeStruct(own.shape, jnp.float32),
        in_specs=[smem] + [vmem] * 4,
        out_specs=vmem,
        compiler_params=pltpu.CompilerParams(vmem_limit_bytes=8 * 1024 * 1024),
        cost_estimate=pl.CostEstimate(flops=5_000_000, bytes_accessed=1_500_000, transcendentals=0),
    )(face_x, own, xup, xdn, speeds_x)


def along_y(face_y, part, own, low, high_, speeds_y):
    rows_x = own.shape[1]
    smem = pl.BlockSpec(memory_space=pltpu.SMEM)
    vmem = pl.BlockSpec(memory_space=pltpu.VMEM)
    return pl.pallas_call(
        along_y_kernel,
        out_shape=jax.ShapeDtypeStruct((rows_x, 4, LEVELS, WIDE), jnp.bfloat16),
        in_specs=[smem] + [vmem] * 5,
        out_specs=vmem,
        compiler_params=pltpu.CompilerParams(vmem_limit_bytes=8 * 1024 * 1024),
        cost_estimate=pl.CostEstimate(flops=5_000_000, bytes_accessed=2_500_000, transcendentals=0),
    )(face_y, part, own, low, high_, speeds_y)


def small(matrix, inputs):
    products = {}

    def product(scale, n):
        if scale == 1.0:
            return inputs[n]
        if (scale, n) not in products:
            products[scale, n] = inputs[n] * scale
        return products[scale, n]

    results = []
    for row in matrix:
        total = None
        for n, value in enumerate(row):
            value = round(float(value), 12)
            if value == 0.0:
                continue
            term = product(abs(value), n)
            if total is None:
                total = term if value > 0 else -term
            else:
                total = total + term if value > 0 else total - term
        results.append(total)
    return results


def trig(function, outs, ins, over):
    return [[function(math.pi * k * n / over) for n in ins] for k in outs]


def cosines(v):
    e = [v[n] + v[12 - n] for n in range(6)] + [v[6]]
    o = [v[n] - v[12 - n] for n in range(6)]
    ee = [e[n] + e[6 - n] for n in range(3)] + [e[3]]
    eo = [e[n] - e[6 - n] for n in range(3)]
    out = [None] * 13
    out[0::4] = small(trig(math.cos, range(4), range(4), 3), ee)
    out[2::4] = small(trig(math.cos, (1, 3, 5), range(3), 6), eo)
    out[1::2] = small(trig(math.cos, (1, 3, 5, 7, 9, 11), range(6), 12), o)
    return out


def sines(v):
    v = [None] + v
    f = [v[n] + v[12 - n] for n in range(1, 6)] + [v[6]]
    g = [None] + [v[n] - v[12 - n] for n in range(1, 6)]
    gp = [g[1] + g[5], g[2] + g[4], g[3]]
    gm = [g[1] - g[5], g[2] - g[4]]
    out = [None] * 11
    out[0::2] = small(trig(math.sin, (1, 3, 5, 7, 9, 11), range(1, 7), 12), f)
    out[1::4] = small(trig(math.sin, (1, 3, 5), (1, 2, 3), 6), gp)
    out[3::4] = small(trig(math.sin, (2, 4), (1, 2), 6), gm)
    return out


def modes_of(x):
    even = [x[0]] + [x[n] + x[VX - n] for n in range(1, 12)] + [x[12]]
    odd = [x[n] - x[VX - n] for n in range(1, 12)]
    return cosines(even) + sines(odd)


def points_of(modes):
    p = cosines(modes[:13])
    q = sines(modes[13:])
    out = [None] * VX
    out[0], out[12] = p[0], p[12]
    for n in range(1, 12):
        out[n] = p[n] + q[n - 1]
        out[VX - n] = p[n] - q[n - 1]
    return out


def split_table():
    table = np.kron(cas_matrix(VY), cas_matrix(VZ)).astype(np.float32)
    table = np.pad(table, ((0, 0), (0, YZ - PLANE)))
    top = table.astype(ml_dtypes.bfloat16)
    low = (table - top.astype(np.float32)).astype(ml_dtypes.bfloat16)
    rest = PLANE - MAIN
    back = np.zeros((DEPTH, YZ), ml_dtypes.bfloat16)
    back[0:MAIN] = top[:MAIN]
    back[MAIN : 2 * MAIN] = low[:MAIN]
    back[2 * MAIN : 2 * MAIN + rest] = top[MAIN:PLANE]
    back[2 * MAIN + rest : 2 * MAIN + 2 * rest] = top[MAIN:PLANE]
    back[2 * MAIN + 128 : 2 * MAIN + 128 + rest] = low[MAIN:PLANE]
    return back


def collide_kernel(
    weights, block, bank, coefs, back, out, g, spec, mixed, lhs, left, gain
):
    cells = block.shape[1] // 2
    per_cell = VX * LEVELS
    blank = jnp.zeros((LEVELS, YZ - PLANE), jnp.float32)

    def plane(cell, a):
        source, i = a // SUB, a % SUB
        wide = [block[source, 2 * cell + half].astype(jnp.float32) for half in range(2)]
        cut = [part[:, i * HALF : (i + 1) * HALF] for part in wide]
        return jnp.concatenate(cut + [blank], axis=1)

    for cell in range(cells):
        for m in range(VX // 2):
            pair = jnp.concatenate([plane(cell, 2 * m), plane(cell, 2 * m + 1)], axis=0)
            at_rows = pl.ds(cell * per_cell + 2 * m * LEVELS, 2 * LEVELS)
            g[at_rows, :] = pair.astype(jnp.bfloat16)

    tiles = YZ // 128
    chunks = ((0, 256), (256, 256), (512, 128))

    edge = jnp.concatenate([g[:, MAIN:], g[:, MAIN:]], axis=1)
    for start, width in chunks:
        cols = pl.ds(start, width)
        total = jnp.dot(edge, back[2 * MAIN :, cols], preferred_element_type=jnp.float32)
        for first in (0, MAIN):
            total = total + jnp.dot(
                g[:, :MAIN], back[pl.ds(first, MAIN), cols], preferred_element_type=jnp.float32
            )
        spec[:, cols] = total

    def rows(base, a, count=LEVELS):
        return pl.ds(base + a * LEVELS, count)

    factor = [
        jnp.broadcast_to(coefs[:, shift : shift + 1], (LEVELS, 128)) for shift in range(LEVELS)
    ]

    def ahead(index):
        base, lanes = index // tiles * per_cell, pl.ds(index % tiles * 128, 128)
        modes = modes_of([spec[rows(base, a), lanes] for a in range(VX)])
        for a in range(VX):
            total = factor[0] * modes[a]
            for shift in range(1, LEVELS):
                total = total + factor[shift] * pltpu.roll(modes[a], shift, 0)
            spec[rows(base, a), lanes] = modes[a]
            mixed[rows(base, a), lanes] = total

    for index in range(cells * tiles):
        ahead(index)

    lane = lax.broadcasted_iota(jnp.int32, (2 * LEVELS, 128), 1)

    def prepare(slot, which, source, base, lanes, t, last):
        factors = [bank[which, pl.ds(k, 1), lanes] for k in range(13)]
        points = points_of(
            [source[rows(base, a), lanes] * factors[a if a < 13 else a - 12] for a in range(VX)]
        )
        for m in range(VX // 2):
            pair = jnp.concatenate([points[2 * m], points[2 * m + 1]], axis=0)
            top = pair.astype(jnp.bfloat16)
            rest = pair - top.astype(jnp.float32)
            at_rows = rows(base, 2 * m, 2 * LEVELS)

            def put(start, value):
                lhs[slot, at_rows, pl.ds(start, 128)] = value

            if last:
                both = jnp.where(lane < PLANE - MAIN, pair, pltpu.roll(rest, 64, 1))
                put(2 * MAIN, both.astype(jnp.bfloat16))
                put(2 * MAIN + 128, top)
            else:
                put(t * 128, rest.astype(jnp.bfloat16))
                put(MAIN + t * 128, top)

    def prepare_all(slot, which, source):
        for cell in range(cells):
            for t in range(tiles):
                base = cell * per_cell
                prepare(slot, which, source, base, pl.ds(t * 128, 128), t, t == tiles - 1)

    def product(slot, start, width):
        cols = pl.ds(start, width)
        total = jnp.dot(
            lhs[slot, :, MAIN:], back[MAIN:, cols], preferred_element_type=jnp.float32
        )
        for first in (0, MAIN):
            total = total + jnp.dot(
                lhs[slot, :, pl.ds(first, MAIN)],
                back[:MAIN, cols],
                preferred_element_type=jnp.float32,
            )
        return total

    for direction in range(2):
        prepare_all(2 * direction, direction, spec)
        prepare_all(2 * direction + 1, 2 + direction, mixed)
        for start, width in chunks:
            left[:, pl.ds(start, width)] = product(2 * direction, start, width)
        for start, width in chunks:
            cols = pl.ds(start, width)
            value = left[:, cols] * product(2 * direction + 1, start, width)
            gain[:, cols] = value if direction == 0 else gain[:, cols] + value
    prepare_all(4, 4, mixed)
    for start, width in chunks:
        loss = product(4, start, width)
        keep = min(width, PLANE - start)
        values = []
        for cell in range(cells):
            at_rows = pl.ds(cell * per_cell, per_cell)
            fields = g[at_rows, pl.ds(start, width)].astype(jnp.float32)
            part = loss[cell * per_cell : (cell + 1) * per_cell]
            values.append(
                fields
                + weights[cell] * (gain[at_rows, pl.ds(start, width)] - fields * part)
            )
        for a in range(VX):
            both = jnp.concatenate(
                [value[a * LEVELS : (a + 1) * LEVELS, :keep] for value in values], axis=0
            )
            at_rows = pl.ds(a * cells * LEVELS, cells * LEVELS)
            out[at_rows, pl.ds(start, keep)] = both.astype(jnp.bfloat16)


def resident_kernel(source, out, sem):
    copy = pltpu.make_async_copy(source, out, sem)
    copy.start()
    copy.wait()


def resident(table):
    return pl.pallas_call(
        resident_kernel,
        out_shape=jax.ShapeDtypeStruct(table.shape, table.dtype),
        in_specs=[pl.BlockSpec(memory_space=pl.ANY)],
        out_specs=pl.BlockSpec(memory_space=pltpu.VMEM),
        scratch_shapes=[pltpu.SemaphoreType.DMA],
        compiler_params=pltpu.CompilerParams(vmem_limit_bytes=8 * 1024 * 1024),
        cost_estimate=pl.CostEstimate(flops=0, bytes_accessed=4_600_000, transcendentals=0),
    )(table)


def collide(weights, block, bank, coefs, back):
    count = block.shape[1] // 2 * VX * LEVELS
    smem = pl.BlockSpec(memory_space=pltpu.SMEM)
    vmem = pl.BlockSpec(memory_space=pltpu.VMEM)
    return pl.pallas_call(
        collide_kernel,
        out_shape=jax.ShapeDtypeStruct((count, PLANE), jnp.bfloat16),
        in_specs=[smem] + [vmem] * 4,
        out_specs=vmem,
        scratch_shapes=[
            pltpu.VMEM((count, YZ), jnp.bfloat16),
            pltpu.VMEM((count, YZ), jnp.float32),
            pltpu.VMEM((count, YZ), jnp.float32),
            pltpu.VMEM((5, count, DEPTH), jnp.bfloat16),
            pltpu.VMEM((count, YZ), jnp.float32),
            pltpu.VMEM((count, YZ), jnp.float32),
        ],
        compiler_params=pltpu.CompilerParams(vmem_limit_bytes=16 * 1024 * 1024),
        cost_estimate=pl.CostEstimate(
            flops=8_000_000_000, bytes_accessed=8_000_000, transcendentals=0
        ),
    )(weights, block, bank, coefs, back)


def ring(count, step):
    return [(i, (i + step) % count) for i in range(count)]


def body(distribution, wall_mask, pair_table, trans_weight, kernels):
    rows_x, rows_y, local_vx, row_width = distribution.shape
    count_x = lax.axis_size("gx")
    count_y = lax.axis_size("gy")
    count_v = lax.axis_size("vert")
    at_v = lax.axis_index("vert")
    forward = at_v >= count_v // 2

    anchor_x = lax.axis_index("gx") * rows_x
    anchor_y = lax.axis_index("gy") * rows_y
    flag = jnp.stack([forward.astype(jnp.int32), anchor_x, anchor_y])
    raw = distribution.transpose(0, 2, 1, 3).reshape(rows_x, SUB, 2, LEVELS, PLANE)
    own, to_low, to_high = split(raw)
    low = lax.ppermute(to_high, "gy", ring(count_y, 1))
    high_ = lax.ppermute(to_low, "gy", ring(count_y, -1))

    index_x = at_v * local_vx + jnp.arange(WIDE, dtype=jnp.int32) // HALF
    speeds_x = jnp.abs(speed(index_x.astype(jnp.float32)))
    upstream, downstream = edges(own)
    send_up, send_down = [], []
    for i in range(count_x):
        for v in range(count_v):
            step = 1 if v >= count_v // 2 else -1
            send_up.append((i * count_v + v, (i + step) % count_x * count_v + v))
            send_down.append((i * count_v + v, (i - step) % count_x * count_v + v))
    xup = lax.ppermute(upstream, ("gx", "vert"), send_up)
    xdn = lax.ppermute(downstream, ("gx", "vert"), send_down)

    openness = open_share(wall_mask)
    own_open = lax.dynamic_slice(openness, (anchor_x + at_v, anchor_y), (1, rows_y))[0]

    speeds_x = jnp.broadcast_to(speeds_x[None], (LEVELS, WIDE))
    speeds_y = jnp.asarray(lane_speeds())
    face_x, face_y = faces(flag, wall_mask, rows_x)
    part = along_x(face_x, own, xup, xdn, speeds_x)
    transported = along_y(face_y, part, own, low, high_, speeds_y)

    back = jnp.asarray(split_table())
    block = lax.all_to_all(transported, "vert", split_axis=0, concat_axis=0, tiled=True)
    entries = jnp.arange(trans_weight.shape[0], dtype=jnp.int32)
    mixing = jnp.sum(
        jnp.where(
            pair_table[:, :, None] == entries[None, None, :], trans_weight[None, None, :], 0.0
        ),
        axis=-1,
    )
    level = np.arange(LEVELS)
    chosen = (level[:, None, None] - level[None, :, None]) % LEVELS == level[None, None, :]
    coefs = jnp.sum(jnp.where(chosen, mixing[:, None, :], 0.0), axis=-1)
    bank = kernels.reshape(kernels.shape[0], VX, PLANE)[:, : VX // 2 + 1]
    twice = np.full((VX // 2 + 1,), 2.0, np.float32)
    twice[0] = twice[VX // 2] = 1.0
    bank = bank * (twice / float(VX * PLANE)).reshape(1, -1, 1)
    bank = jnp.pad(bank, ((0, 0), (0, 0), (0, YZ - PLANE)))
    updated = collide(
        collide_step * own_open, block, bank, coefs, back
    )
    updated = updated.reshape(VX, 2, row_width)
    result = lax.all_to_all(updated, "vert", split_axis=0, concat_axis=0, tiled=True)
    return result.reshape(rows_x, local_vx, 2, row_width).transpose(0, 2, 1, 3)


def solution(mesh):
    in_specs = (P("gx", "gy", "vert", None), P(), P(), P(), P())
    out_specs = P("gx", "gy", "vert", None)
    return jax.shard_map(body, mesh=mesh, in_specs=in_specs, out_specs=out_specs, check_vma=False)
```
